512 devices in a mesh: dp: 128 (over z, y, core), head: 4 (over x).
Axes of the slice: x: 4, y: 4, z: 16, core: 2. Of those that a mesh axis runs over, the one named last changes fastest.
Arguments:
- tile_features: bfloat16 [45056, 768], P('dp')
- tile_weight: bfloat16 [768, 768], replicated, may hold values from -0.21875 to 0.21875
- tile_bias: float32 [768], replicated, may hold values from -3 to 3
- query_weight: bfloat16 [768, 768], P(None, 'head'), may hold values from -1.25 to 1.25
- key_weight: bfloat16 [768, 768], P(None, 'head'), may hold values from -0.21875 to 0.21875
- value_weight: bfloat16 [768, 768], P(None, 'head'), may hold values from -0.21875 to 0.21875
- output_weight: bfloat16 [768, 768], P('head'), may hold values from -0.21875 to 0.21875
- tile_region: int32 [45056], replicated, may hold values from 0 to 255, as said below
- region_block: int32 [256], replicated, may hold values from 0 to 255, as said below
- region_count: int32 [256], replicated, may hold values from 96 to 256, as said below
Outputs:
- tile_mixed: bfloat16 [256, 256, 768], P('dp', None, 'head')
- region_out: bfloat16 [256, 768], P('dp', 'head')
The draws below stay inside these ranges and needn't reach their ends.
Inputs may be any that keep to these rules, and one draw needn't show every extreme that they name: region_block is a permutation of the blocks. region_count[r] is the number of tiles t with tile_region[t] = r; one index of dp holds at most 2 tiles of one region, and some region reaches it on every index. `tile_region`: each region has 96 to 256 tiles.
All inputs are finite; a program needn't handle non-finite values.
Results may differ from the reference program's by a relative error of at most 0.018.
The reference program's roundings to bfloat16 on the way (of `embedded`, `slotted`, `queries`, `weights` and `pooled`) count: a program that leaves them out, or rounds other values in their place, can miss the bound.
Values may be sent and summed in bfloat16 or wider, within the bound.
A program may use at most 64 MiB of HBM per device.

```python
import jax
import jax.numpy as jnp
from jax import lax

D = 768
HEADS = 12
SLOTS = 256
HD = 64
TILE_DEV = 352
TILES = 45056
REGIONS = 256
SUB = 2
N_DP = 128


def region_layout(key):
    first_key, order_key, block_key, shuffle_key = jax.random.split(key, 4)
    half = REGIONS // 2
    lowest = 3 * SLOTS // 8
    first = lowest + jax.random.randint(first_key, (half,), 0, SLOTS - lowest + 1)
    first = first.at[0].set(SLOTS)
    counts = jnp.concatenate([first, 11 * SLOTS // 8 - first]).astype(jnp.int32)
    counts = counts[jax.random.permutation(order_key, REGIONS)]
    blocks = jax.random.permutation(block_key, REGIONS).astype(jnp.int32)
    by_block = jnp.argsort(blocks, stable=True).astype(jnp.int32)
    ends = jnp.cumsum(counts[by_block])
    position = jnp.arange(TILES, dtype=jnp.int32)
    which = jnp.searchsorted(ends, position, side='right').astype(jnp.int32)
    sorted_regions = by_block[which]
    spread = sorted_regions.reshape(TILE_DEV, N_DP).T
    spread = jax.random.permutation(shuffle_key, spread, axis=1, independent=True)
    return (counts, blocks, spread.reshape(TILES).astype(jnp.int32))


def draw_tile_region(key, part):
    counts, blocks, regions = region_layout(key)
    return regions


def draw_region_block(key, part):
    counts, blocks, regions = region_layout(key)
    return blocks


def draw_region_count(key, part):
    counts, blocks, regions = region_layout(key)
    return counts


def draw_tile_features(key, part):
    key = jax.random.fold_in(key, 5)
    base_key = jax.random.fold_in(key, 0)
    values = jnp.clip(jax.random.normal(base_key, (TILES, D), jnp.float32), -6.0, 6.0)
    return values.astype(jnp.bfloat16)


def level_of(rng, extent, pieces, low, largest):
    factor_of = 1.0
    for axis_at, blocks in pieces:
        steps = jax.random.uniform(jax.random.fold_in(jax.random.fold_in(rng, 6), axis_at), (blocks,), jnp.float32, low / len(pieces), largest / len(pieces))
        factor_of = factor_of * jnp.repeat(jnp.exp(steps), extent[axis_at] // blocks).reshape((-1,) + (1,) * (len(extent) - 1 - axis_at))
    return factor_of


def noise(stream_key, extent, width, limit, shards=(), held_as=jnp.bfloat16):
    loudness = level_of(stream_key, extent, shards, -0.22, 0.18) if shards else 1.0
    array = jax.random.normal(stream_key, extent, jnp.float32) * width * loudness
    return jnp.minimum(jnp.maximum(array, -limit), limit).astype(held_as)


def setup_inputs(seed: int = 0) -> dict:
    streams_of = jax.random.split(jax.random.key(seed), 11)
    tile_features = draw_tile_features(jax.random.fold_in(streams_of[10], 71), 0)
    tile_weight = noise(streams_of[1], (D, D), D ** -0.5, 0.21875)
    tile_bias = noise(streams_of[2], (D,), 0.5, 3.0, (), jnp.float32)
    query_weight = noise(streams_of[3], (D, D), 0.2, 1.25, ((1, 4),))
    key_weight = noise(streams_of[4], (D, D), D ** -0.5, 0.21875, ((1, 4),))
    value_weight = noise(streams_of[5], (D, D), D ** -0.5, 0.21875, ((1, 4),))
    output_weight = noise(streams_of[6], (D, D), D ** -0.5, 0.21875, ((0, 4),))
    tile_region = draw_tile_region(jax.random.fold_in(streams_of[10], 71), 0)
    region_block = draw_region_block(jax.random.fold_in(streams_of[10], 71), 0)
    region_count = draw_region_count(jax.random.fold_in(streams_of[10], 71), 0)
    return {"tile_features": tile_features, "tile_weight": tile_weight, "tile_bias": tile_bias, "query_weight": query_weight, "key_weight": key_weight, "value_weight": value_weight, "output_weight": output_weight, "tile_region": tile_region, "region_block": region_block, "region_count": region_count}


def tile_ranks(local_regions):
    count = local_regions.shape[0]
    order = lax.iota(jnp.int32, count)
    same = local_regions[:, None] == local_regions[None, :]
    earlier = order[None, :] < order[:, None]
    return jnp.sum((same & earlier).astype(jnp.int32), axis=1)


def attend_block(packed):
    queries, keys_in, vals_in, live = packed
    scores = jnp.einsum("qhe,khe->hqk", queries.astype(jnp.float32), keys_in.astype(jnp.float32)) * (HD ** -0.5)
    scores = jnp.where(live[None, None, :], scores, -1e30)
    top = jnp.max(scores, axis=-1, keepdims=True)
    weights = jnp.exp(scores - top)
    weights = (weights / jnp.sum(weights, axis=-1, keepdims=True)).astype(jnp.bfloat16)
    mixed = jnp.einsum("hqk,khe->qhe", weights.astype(jnp.float32), vals_in.astype(jnp.float32))
    mixed = jnp.where(live[:, None, None], mixed, 0.0)
    return mixed.reshape(SLOTS, D).astype(jnp.bfloat16)


def reference(tile_features, tile_weight, tile_bias, query_weight, key_weight, value_weight, output_weight, tile_region, region_block, region_count):
    hidden = jnp.dot(tile_features, tile_weight, preferred_element_type=jnp.float32) + tile_bias
    embedded = jax.nn.gelu(hidden, approximate=True).astype(jnp.bfloat16)
    ranks = lax.map(tile_ranks, tile_region.reshape(N_DP, TILE_DEV)).reshape(TILES)
    source = (jnp.arange(TILES) // TILE_DEV).astype(jnp.int32)
    flat = (region_block[tile_region] * SLOTS + source * SUB + ranks).astype(jnp.int32)
    slotted = jnp.zeros((REGIONS * SLOTS, D), jnp.bfloat16).at[flat].set(embedded)
    live = jnp.zeros((REGIONS * SLOTS,), jnp.bool_).at[flat].set(True)
    queries = jnp.dot(slotted, query_weight, preferred_element_type=jnp.float32).astype(jnp.bfloat16)
    keys_all = jnp.dot(slotted, key_weight, preferred_element_type=jnp.float32).astype(jnp.bfloat16)
    vals_all = jnp.dot(slotted, value_weight, preferred_element_type=jnp.float32).astype(jnp.bfloat16)
    shape = (REGIONS, SLOTS, HEADS, HD)
    tile_mixed = lax.map(attend_block, (queries.reshape(shape), keys_all.reshape(shape), vals_all.reshape(shape), live.reshape(REGIONS, SLOTS)))
    block_region = jnp.zeros((REGIONS,), jnp.int32).at[region_block].set(jnp.arange(REGIONS).astype(jnp.int32))
    counts = region_count[block_region].astype(jnp.float32)
    pooled = (jnp.sum(tile_mixed.astype(jnp.float32), axis=1) / counts[:, None]).astype(jnp.bfloat16)
    region_out = jnp.dot(pooled, output_weight, preferred_element_type=jnp.float32).astype(jnp.bfloat16)
    return tile_mixed, region_out
```

```python
import functools

import jax
import jax.numpy as jnp
from jax import lax
from jax.experimental import pallas as pl
from jax.experimental.pallas import tpu as pltpu
from jax.sharding import PartitionSpec as P

D = 768
SLOTS = 256
HD = 64
COLS = 192
TILE = 352
PAD = 384
NZ, NG, NX = 16, 8, 4
EMPTY = -8.0
MESH = pl.DeviceIdType.MESH
F32 = jnp.float32
BF16 = jnp.bfloat16
LAST = (((1,), (1,)), ((), ()))
GROUPS = ((0, 4), (4, 4), (8, 4), (12, 4))


def delta_of(p):
    if p == 0:
        return 0
    k = 8 - p // 2
    return k if p % 2 == 0 else 16 - k


def iota(shape, dim):
    return lax.broadcasted_iota(jnp.int32, shape, dim)


def kernel(
    feat, w, bias, wq, wk, wv, wo, reg, blk, cnt,
    mixed_out, region_out,
    f_v, w_v, bias_v, wq_v, wk_v, wv_v, wo_v, reg_v, blk_v, cnt_v,
    e_v, g_v, z_v, a_v, q_v, k_v, o_v, s_v, r_v,
    in_sem, own_sem, gs_sem, gr_sem, zs_sem, zr_sem, xs_sem, xr_sem, ps_sem, pr_sem, out_sem,
):
    dp = lax.axis_index("dp")
    h = lax.axis_index("head")
    z = dp // NG
    g = dp % NG

    first_row = (dp * TILE) // 128
    lane_off = (dp * TILE) % 128
    reg_base = pl.multiple_of(jnp.minimum((first_row // 8) * 8, TILE - 16), 8)
    loads = [
        pltpu.make_async_copy(reg.at[pl.ds(reg_base, 16)], reg_v, in_sem.at[0]),
        pltpu.make_async_copy(blk, blk_v, in_sem.at[1]),
        pltpu.make_async_copy(feat, f_v.at[pl.ds(0, TILE)], in_sem.at[2]),
        pltpu.make_async_copy(w, w_v, in_sem.at[3]),
        pltpu.make_async_copy(bias, bias_v, in_sem.at[4]),
        pltpu.make_async_copy(wq, wq_v, in_sem.at[5]),
        pltpu.make_async_copy(wk, wk_v, in_sem.at[6]),
        pltpu.make_async_copy(wv, wv_v, in_sem.at[7]),
        pltpu.make_async_copy(wo, wo_v, in_sem.at[8]),
        pltpu.make_async_copy(cnt, cnt_v, in_sem.at[9]),
    ]
    for load in loads:
        load.start()

    barrier = pltpu.get_barrier_semaphore()
    for o in range(1, NG):
        pl.semaphore_signal(
            barrier, inc=1, device_id={"dp": z * NG + (g + o) % NG, "head": h}, device_id_type=MESH
        )
    for o in range(1, NZ):
        pl.semaphore_signal(
            barrier, inc=1, device_id={"dp": ((z + o) % NZ) * NG + g, "head": h}, device_id_type=MESH
        )
    for o in range(1, NX):
        pl.semaphore_signal(
            barrier, inc=1, device_id={"dp": dp, "head": (h + o) % NX}, device_id_type=MESH
        )

    f_v[pl.ds(TILE, PAD - TILE), :] = jnp.zeros((PAD - TILE, D), BF16)
    upper = (iota((PAD, PAD), 0) < iota((PAD, PAD), 1)).astype(F32).astype(BF16)
    loads[0].wait()
    loads[1].wait()
    parts = []
    for i in range(4):
        at = jnp.minimum(first_row + i, TILE - 1) - reg_base
        parts.append(reg_v[pl.ds(at, 1), :])
    line = jnp.broadcast_to(jnp.concatenate(parts, axis=1), (8, 512))
    line = pltpu.roll(line, (512 - lane_off) % 512, 1)[:, :PAD]
    in_range = iota((8, PAD), 1) < TILE
    line = jnp.where(in_range, line, -1)
    hot = (iota((256, PAD), 0) == line[0:1, :]).astype(F32)
    hot16 = hot.astype(BF16)
    block_row = jnp.broadcast_to(blk_v[...].astype(F32), (8, 256)).astype(BF16)
    block = jnp.dot(block_row, hot16, preferred_element_type=F32)
    before = jnp.dot(hot16, upper, preferred_element_type=F32)
    rank = jnp.sum(before * hot, axis=0, keepdims=True)
    code = jnp.where(in_range[0:1, :], block[0:1, :] * 2.0 + rank, -1.0)
    row = iota((128, PAD), 0)
    target = (4 * ((row % NZ) * NG + row // NZ) + h).astype(F32)
    pick = (code == target).astype(F32)
    live = jnp.sum(pick, axis=1, keepdims=True)
    loads[2].wait()
    x = jnp.dot(pick.astype(BF16), f_v[...], preferred_element_type=F32).astype(BF16)
    loads[3].wait()
    loads[4].wait()
    hidden = jnp.dot(x, w_v[...], preferred_element_type=F32) + bias_v[...]
    embedded = jax.nn.gelu(hidden, approximate=True)
    embedded = jnp.where(live > 0.5, embedded, EMPTY).astype(BF16)
    e_v[...] = embedded.reshape(NG, NZ, D)

    pl.semaphore_wait(barrier, NG + NZ + NX - 3)

    g_sends = []
    for o in range(1, NG):
        to = (g + o) % NG
        copy = pltpu.make_async_remote_copy(
            src_ref=e_v.at[to],
            dst_ref=g_v.at[g],
            send_sem=gs_sem.at[o - 1],
            recv_sem=gr_sem.at[o - 1],
            device_id={"dp": z * NG + to, "head": h},
            device_id_type=MESH,
        )
        copy.start()
        g_sends.append(copy)
    g_v[pl.ds(g, 1)] = e_v[pl.ds(g, 1)]
    order = (iota((128, 128), 1) == (iota((128, 128), 0) % NG) * NZ + iota((128, 128), 0) // NG)
    order = order.astype(F32).astype(BF16)
    for copy in g_sends:
        copy.wait_recv()
    by_z = jnp.dot(order, g_v[...].reshape(128, D), preferred_element_type=F32).astype(BF16)
    z_v[...] = by_z.reshape(NZ, NG, D)

    z_sends = {}
    for p in range(1, NZ):
        to = (z + NZ - delta_of(p)) % NZ
        copy = pltpu.make_async_remote_copy(
            src_ref=z_v.at[to],
            dst_ref=a_v.at[h, p],
            send_sem=zs_sem.at[p],
            recv_sem=zr_sem.at[p],
            device_id={"dp": to * NG + g, "head": h},
            device_id_type=MESH,
        )
        copy.start()
        z_sends[p] = copy
    own = pltpu.make_async_copy(z_v.at[z], a_v.at[h, 0], own_sem)
    own.start()

    x_sends = []
    for n, (start, size) in enumerate(GROUPS):
        for p in range(start, start + size):
            if p == 0:
                own.wait()
            else:
                z_sends[p].wait_recv()
        sends = []
        for o in range(1, NX):
            copy = pltpu.make_async_remote_copy(
                src_ref=a_v.at[h, pl.ds(start, size)],
                dst_ref=a_v.at[h, pl.ds(start, size)],
                send_sem=xs_sem.at[n, o - 1],
                recv_sem=xr_sem.at[n, o - 1],
                device_id={"dp": dp, "head": (h + o) % NX},
                device_id_type=MESH,
            )
            copy.start()
            sends.append(copy)
        x_sends.append(sends)

    loads[5].wait()
    loads[6].wait()
    for n, (start, size) in enumerate(GROUPS):
        for copy in x_sends[n]:
            copy.wait_recv()
        rows = a_v[:, pl.ds(start, size)].reshape(NX * size * NG, D)
        place = pl.ds(start * NG, size * NG)
        for weight, kept in ((wq_v, q_v), (wk_v, k_v)):
            made = lax.dot_general(rows, weight[...], LAST, preferred_element_type=F32)
            kept[:, place] = made.astype(BF16).reshape(NX, size * NG, COLS)

    lane = iota((SLOTS, COLS), 1)
    at = iota((SLOTS, SLOTS), 0)
    slot = iota((SLOTS, SLOTS), 1)
    place = (at % 128) // NG
    k_off = 8 - place // 2
    off = jnp.where(place % 2 == 0, k_off, NZ - k_off)
    off = jnp.where(place == 0, 0, off)
    to_slot = (((z + off) % NZ) * NG + at % NG) * 2 + at // 128
    perm = (slot == to_slot).astype(F32)
    ones = jnp.ones((8, SLOTS), BF16)
    loads[7].wait()
    sums = []
    outs = []
    for j in range(2):
        queries = q_v[2 * j : 2 * j + 2].reshape(SLOTS, COLS)
        keys = k_v[2 * j : 2 * j + 2].reshape(SLOTS, COLS)
        rows = a_v[2 * j : 2 * j + 2].reshape(SLOTS, D)
        vals = lax.dot_general(wv_v[...], rows, LAST, preferred_element_type=F32).astype(BF16)
        alive = rows[:, 0:1].astype(F32) > -4.0
        shut = jnp.where(alive, 0.0, -1e30)
        parts = []
        for n in range(3):
            mine = (lane >= n * HD) & (lane < (n + 1) * HD)
            head_keys = jnp.where(mine, keys, jnp.zeros_like(keys))
            scores = lax.dot_general(head_keys, queries, LAST, preferred_element_type=F32)
            scores = scores * (HD ** -0.5) + shut
            top = jnp.max(scores, axis=0, keepdims=True)
            weights = jnp.exp(scores - top)
            inverse = 1.0 / jnp.sum(weights, axis=0, keepdims=True)
            part = jnp.dot(
                vals[n * HD : (n + 1) * HD], weights.astype(BF16), preferred_element_type=F32
            )
            parts.append((part * inverse).astype(BF16))
        mixed = jnp.concatenate(parts, axis=0)
        ordered = jnp.where(alive, perm, 0.0).astype(BF16)
        result = jnp.dot(mixed, ordered, preferred_element_type=F32).astype(BF16)
        o_v[j] = result
        out = pltpu.make_async_copy(o_v.at[j], mixed_out.at[j], out_sem.at[j])
        out.start()
        outs.append(out)
        sums.append(lax.dot_general(ones, result, LAST, preferred_element_type=F32)[0:1])

    loads[8].wait()
    loads[9].wait()
    pooled = []
    for j in range(2):
        here = blk_v[...] == dp * 2 + j
        count = jnp.sum(jnp.where(here, cnt_v[...].astype(F32), 0.0), axis=1, keepdims=True)
        pooled.append(sums[j] / count)
    pooled = jnp.concatenate(pooled + [jnp.zeros((6, COLS), F32)], axis=0).astype(BF16)
    partial = jnp.dot(pooled, wo_v[...], preferred_element_type=F32)
    for i in range(NX):
        s_v[i, :, 0:COLS] = partial[:, i * COLS : (i + 1) * COLS]
        s_v[i, :, COLS:256] = jnp.zeros((8, 256 - COLS), F32)
    p_sends = []
    for o in range(1, NX):
        to = (h + o) % NX
        copy = pltpu.make_async_remote_copy(
            src_ref=s_v.at[to],
            dst_ref=r_v.at[o - 1],
            send_sem=ps_sem.at[o - 1],
            recv_sem=pr_sem.at[o - 1],
            device_id={"dp": dp, "head": to},
            device_id_type=MESH,
        )
        copy.start()
        p_sends.append(copy)
    for copy in g_sends:
        copy.wait_send()
    for copy in z_sends.values():
        copy.wait_send()
    for sends in x_sends:
        for copy in sends:
            copy.wait_send()
    own_part = s_v[h]
    for copy in p_sends:
        copy.wait_recv()
    everything = own_part + r_v[0] + r_v[1] + r_v[2]
    region_out[...] = everything[0:2, 0:COLS].astype(BF16)
    for copy in p_sends:
        copy.wait_send()
    for out in outs:
        out.wait()


def local(
    tile_features, tile_weight, tile_bias, query_weight, key_weight, value_weight, output_weight,
    tile_region, region_block, region_count,
):
    dma = pltpu.SemaphoreType.DMA
    anywhere = pl.BlockSpec(memory_space=pl.ANY)
    groups = len(GROUPS)
    mixed, region = pl.pallas_call(
        kernel,
        out_shape=(
            jax.ShapeDtypeStruct((2, COLS, SLOTS), BF16),
            jax.ShapeDtypeStruct((2, COLS), BF16),
        ),
        in_specs=[anywhere] * 10,
        out_specs=(anywhere, pl.BlockSpec(memory_space=pltpu.VMEM)),
        scratch_shapes=[
            pltpu.VMEM((PAD, D), BF16),
            pltpu.VMEM((D, D), BF16),
            pltpu.VMEM((1, D), F32),
            pltpu.VMEM((COLS, D), BF16),
            pltpu.VMEM((COLS, D), BF16),
            pltpu.VMEM((COLS, D), BF16),
            pltpu.VMEM((COLS, D), BF16),
            pltpu.VMEM((16, 128), jnp.int32),
            pltpu.VMEM((1, 256), jnp.int32),
            pltpu.VMEM((1, 256), jnp.int32),
            pltpu.VMEM((NG, NZ, D), BF16),
            pltpu.VMEM((NG, NZ, D), BF16),
            pltpu.VMEM((NZ, NG, D), BF16),
            pltpu.VMEM((NX, NZ, NG, D), BF16),
            pltpu.VMEM((NX, 128, COLS), BF16),
            pltpu.VMEM((NX, 128, COLS), BF16),
            pltpu.VMEM((2, COLS, SLOTS), BF16),
            pltpu.VMEM((NX, 8, 256), F32),
            pltpu.VMEM((NX - 1, 8, 256), F32),
            dma((10,)),
            dma,
            dma((NG - 1,)),
            dma((NG - 1,)),
            dma((NZ,)),
            dma((NZ,)),
            dma((groups, NX - 1)),
            dma((groups, NX - 1)),
            dma((NX - 1,)),
            dma((NX - 1,)),
            dma((2,)),
        ],
        compiler_params=pltpu.CompilerParams(
            collective_id=0, has_side_effects=True, vmem_limit_bytes=60 * 1024 * 1024
        ),
        name="regroup_attend",
    )(
        tile_features, tile_weight, tile_bias.reshape(1, D), query_weight.T, key_weight.T, value_weight.T,
        output_weight, tile_region.reshape(TILE, 128), region_block.reshape(1, 256),
        region_count.reshape(1, 256),
    )
    return mixed.transpose(0, 2, 1), region


def solution(mesh):
    in_specs = (
        P("dp", None),
        P(),
        P(),
        P(None, "head"),
        P(None, "head"),
        P(None, "head"),
        P("head", None),
        P(),
        P(),
        P(),
    )
    out_specs = (P("dp", None, "head"), P("dp", "head"))
    return jax.shard_map(local, mesh=mesh, in_specs=in_specs, out_specs=out_specs, check_vma=False)
```

```python
import functools

import jax
import jax.numpy as jnp
from jax import lax
from jax.experimental import pallas as pl
from jax.experimental.pallas import tpu as pltpu
from jax.sharding import PartitionSpec as P

D = 768
SLOTS = 256
HD = 64
COLS = 192
TILE = 352
PAD = 384
NZ, NG, NX = 16, 8, 4
EMPTY = -8.0
MESH = pl.DeviceIdType.MESH
F32 = jnp.float32
BF16 = jnp.bfloat16
LAST = (((1,), (1,)), ((), ()))
CHUNK = 4
CHUNKS = NZ // CHUNK
OFFSETS = (0, 1, 15, 2, 14, 3, 13, 4, 12, 5, 11, 6, 10, 7, 9, 8)


def iota(shape, dim):
    return lax.broadcasted_iota(jnp.int32, shape, dim)


def kernel(
    feat, w, bias, wq, wk, wv, wo, reg, blk, cnt,
    mixed_out, region_out,
    f_v, w_v, bias_v, wq_v, wk_v, wv_v, wo_v, reg_v, blk_v, cnt_v,
    e_v, z_v, c_v, a_v, perm_v, o_v, s_v, r_v,
    in_sem, own_sem, zs_sem, zr_sem, xs_sem, xr_sem, ps_sem, pr_sem, out_sem,
):
    dp = lax.axis_index("dp")
    h = lax.axis_index("head")
    z = dp // NG
    g = dp % NG
    y = g // 2
    core = g % 2

    first_row = (dp * TILE) // 128
    lane_off = (dp * TILE) % 128
    reg_base = pl.multiple_of(jnp.minimum((first_row // 8) * 8, TILE - 16), 8)
    loads = [
        pltpu.make_async_copy(reg.at[pl.ds(reg_base, 16)], reg_v, in_sem.at[0]),
        pltpu.make_async_copy(blk, blk_v, in_sem.at[1]),
        pltpu.make_async_copy(feat, f_v.at[pl.ds(0, TILE)], in_sem.at[2]),
        pltpu.make_async_copy(w, w_v, in_sem.at[3]),
        pltpu.make_async_copy(bias, bias_v, in_sem.at[4]),
        pltpu.make_async_copy(wq, wq_v, in_sem.at[5]),
        pltpu.make_async_copy(wk, wk_v, in_sem.at[6]),
        pltpu.make_async_copy(wv, wv_v, in_sem.at[7]),
        pltpu.make_async_copy(wo, wo_v, in_sem.at[8]),
        pltpu.make_async_copy(cnt, cnt_v, in_sem.at[9]),
    ]
    for load in loads:
        load.start()

    barrier = pltpu.get_barrier_semaphore()
    for o in range(NG):
        source = (g + o) % NG
        if o == 0:
            @pl.when(y != h)
            def _():
                pl.semaphore_signal(
                    barrier, inc=1, device_id={"dp": dp, "head": y}, device_id_type=MESH
                )
        else:
            pl.semaphore_signal(
                barrier, inc=1, device_id={"dp": z * NG + source, "head": y}, device_id_type=MESH
            )
    for o in range(1, NZ):
        pl.semaphore_signal(
            barrier, inc=1, device_id={"dp": ((z + o) % NZ) * NG + g, "head": h}, device_id_type=MESH
        )
    for o in range(1, NX):
        pl.semaphore_signal(
            barrier, inc=1, device_id={"dp": dp, "head": (h + o) % NX}, device_id_type=MESH
        )

    f_v[pl.ds(TILE, PAD - TILE), :] = jnp.zeros((PAD - TILE, D), BF16)
    upper = (iota((PAD, PAD), 0) < iota((PAD, PAD), 1)).astype(F32).astype(BF16)
    loads[0].wait()
    loads[1].wait()
    parts = []
    for i in range(4):
        at = jnp.minimum(first_row + i, TILE - 1) - reg_base
        parts.append(reg_v[pl.ds(at, 1), :])
    line = jnp.broadcast_to(jnp.concatenate(parts, axis=1), (8, 512))
    line = pltpu.roll(line, (512 - lane_off) % 512, 1)[:, :PAD]
    in_range = iota((8, PAD), 1) < TILE
    line = jnp.where(in_range, line, -1)
    hot = (iota((256, PAD), 0) == line[0:1, :]).astype(F32)
    hot16 = hot.astype(BF16)
    block_row = jnp.broadcast_to(blk_v[...].astype(F32), (8, 256)).astype(BF16)
    block = jnp.dot(block_row, hot16, preferred_element_type=F32)
    before = jnp.dot(hot16, upper, preferred_element_type=F32)
    rank = jnp.sum(before * hot, axis=0, keepdims=True)
    code = jnp.where(in_range[0:1, :], block[0:1, :] * 2.0 + rank, -1.0)
    row = iota((128, PAD), 0)
    target = (32 * (row // NG) + 8 * h + row % NG).astype(F32)
    pick = (code == target).astype(F32)
    live = jnp.sum(pick, axis=1, keepdims=True)
    loads[2].wait()
    x = jnp.dot(pick.astype(BF16), f_v[...], preferred_element_type=F32).astype(BF16)
    loads[3].wait()
    loads[4].wait()
    hidden = jnp.dot(x, w_v[...], preferred_element_type=F32) + bias_v[...].reshape(1, D)
    embedded = jax.nn.gelu(hidden, approximate=True)
    embedded = jnp.where(live > 0.5, embedded, EMPTY).astype(BF16)
    e_v[...] = embedded.reshape(NZ, NG, D)

    pl.semaphore_wait(barrier, NG + NZ - 1 + NX - 1 - (y == h).astype(jnp.int32))

    z_sends = {}
    for p in range(1, NZ):
        to = (z + NZ - OFFSETS[p]) % NZ
        copy = pltpu.make_async_remote_copy(
            src_ref=e_v.at[to],
            dst_ref=z_v.at[p],
            send_sem=zs_sem.at[p],
            recv_sem=zr_sem.at[p],
            device_id={"dp": to * NG + g, "head": h},
            device_id_type=MESH,
        )
        copy.start()
        z_sends[p] = copy
    own = pltpu.make_async_copy(e_v.at[z], z_v.at[0], own_sem)
    own.start()

    at = iota((SLOTS, SLOTS), 0)
    slot = iota((SLOTS, SLOTS), 1)
    place = (at // 8 % CHUNKS) * CHUNK + at % CHUNK
    off = jnp.zeros((SLOTS, SLOTS), jnp.int32)
    for p in range(1, NZ):
        off = jnp.where(place == p, OFFSETS[p], off)
    to_slot = (((z + off) % NZ) * NG + at // 32) * 2 + at // CHUNK % 2
    perm_v[...] = (slot == to_slot).astype(F32).astype(BF16)

    rows = 8 * CHUNK
    out_row = iota((rows, rows), 0)
    in_row = (out_row % CHUNK) * 8 + out_row // 8 % 2 * 2 + out_row // 16 * 4 + out_row // CHUNK % 2
    order = (iota((rows, rows), 1) == in_row).astype(F32).astype(BF16)
    x_sends = []
    local_sends = []
    for n in range(CHUNKS):
        for p in range(n * CHUNK, (n + 1) * CHUNK):
            if p == 0:
                own.wait()
            else:
                z_sends[p].wait_recv()
        arrived = z_v[n * CHUNK : (n + 1) * CHUNK].reshape(rows, D)
        turned = jnp.dot(order, arrived, preferred_element_type=F32).astype(BF16)
        c_v[n] = turned.reshape(2, 2, 2 * CHUNK, D)
        for o in (2, 1, 3, 0):
            for oc in (1, 0):
                to = (h + o) % NX
                to_core = (core + oc) % 2
                copy = pltpu.make_async_remote_copy(
                    src_ref=c_v.at[n, to_core],
                    dst_ref=a_v.at[:, g, n],
                    send_sem=xs_sem.at[n, o, oc],
                    recv_sem=xr_sem.at[n, g],
                    device_id={"dp": z * NG + h * 2 + to_core, "head": to},
                    device_id_type=MESH,
                )
                if o == 0 and oc == 0:
                    here = pltpu.make_async_copy(
                        c_v.at[n, to_core], a_v.at[:, g, n], xr_sem.at[n, g]
                    )
                    pl.when(y == h)(here.start)
                    pl.when(y != h)(copy.start)
                    local_sends.append(copy)
                else:
                    copy.start()
                    x_sends.append(copy)

    loads[5].wait()
    loads[6].wait()
    loads[7].wait()
    for n in range(CHUNKS):
        for source in range(NG):
            landed = a_v.at[:, source, n]
            pltpu.make_async_copy(landed, landed, xr_sem.at[n, source]).wait()

    lane = iota((SLOTS, COLS), 1)
    ones = jnp.ones((8, SLOTS), BF16)
    sums = []
    outs = []
    for j in range(2):
        rows = a_v[j].reshape(SLOTS, D)
        queries = lax.dot_general(rows, wq_v[...], LAST, preferred_element_type=F32).astype(BF16)
        keys = lax.dot_general(rows, wk_v[...], LAST, preferred_element_type=F32).astype(BF16)
        vals = lax.dot_general(wv_v[...], rows, LAST, preferred_element_type=F32).astype(BF16)
        alive = rows[:, 0:1].astype(F32) > -4.0
        shut = jnp.where(alive, 0.0, -1e30)
        parts = []
        for n in range(3):
            mine = (lane >= n * HD) & (lane < (n + 1) * HD)
            head_keys = jnp.where(mine, keys, jnp.zeros_like(keys))
            scores = lax.dot_general(head_keys, queries, LAST, preferred_element_type=F32)
            scores = scores * (HD ** -0.5) + shut
            top = jnp.max(scores, axis=0, keepdims=True)
            weights = jnp.exp(scores - top)
            inverse = 1.0 / jnp.sum(weights, axis=0, keepdims=True)
            part = jnp.dot(
                vals[n * HD : (n + 1) * HD], weights.astype(BF16), preferred_element_type=F32
            )
            parts.append((part * inverse).astype(BF16))
        mixed = jnp.concatenate(parts, axis=0)
        ordered = jnp.where(alive, perm_v[...].astype(F32), 0.0).astype(BF16)
        result = jnp.dot(mixed, ordered, preferred_element_type=F32).astype(BF16)
        o_v[j] = result
        out = pltpu.make_async_copy(o_v.at[j], mixed_out.at[j], out_sem.at[j])
        out.start()
        outs.append(out)
        sums.append(lax.dot_general(ones, result, LAST, preferred_element_type=F32)[0:1])

    loads[8].wait()
    loads[9].wait()
    pooled = []
    for j in range(2):
        here = blk_v[...] == dp * 2 + j
        count = jnp.sum(jnp.where(here, cnt_v[...].astype(F32), 0.0), axis=1, keepdims=True)
        pooled.append(sums[j] / count)
    pooled = jnp.concatenate(pooled + [jnp.zeros((6, COLS), F32)], axis=0).astype(BF16)
    partial = jnp.dot(pooled, wo_v[...], preferred_element_type=F32)
    for i in range(NX):
        s_v[i, :, 0:COLS] = partial[:, i * COLS : (i + 1) * COLS]
        s_v[i, :, COLS:256] = jnp.zeros((8, 256 - COLS), F32)
    p_sends = []
    for o in range(1, NX):
        to = (h + o) % NX
        copy = pltpu.make_async_remote_copy(
            src_ref=s_v.at[to],
            dst_ref=r_v.at[o - 1],
            send_sem=ps_sem.at[o - 1],
            recv_sem=pr_sem.at[o - 1],
            device_id={"dp": dp, "head": to},
            device_id_type=MESH,
        )
        copy.start()
        p_sends.append(copy)
    for copy in z_sends.values():
        copy.wait_send()
    for copy in x_sends:
        copy.wait_send()
    for copy in local_sends:
        pl.when(y != h)(copy.wait_send)
    own_part = s_v[h]
    for copy in p_sends:
        copy.wait_recv()
    everything = own_part + r_v[0] + r_v[1] + r_v[2]
    region_out[...] = everything[0:2, 0:COLS].astype(BF16)
    for copy in p_sends:
        copy.wait_send()
    for out in outs:
        out.wait()


def local(
    tile_features, tile_weight, tile_bias, query_weight, key_weight, value_weight, output_weight,
    tile_region, region_block, region_count,
):
    dma = pltpu.SemaphoreType.DMA
    anywhere = pl.BlockSpec(memory_space=pl.ANY)
    mixed, region = pl.pallas_call(
        kernel,
        out_shape=(
            jax.ShapeDtypeStruct((2, COLS, SLOTS), BF16),
            jax.ShapeDtypeStruct((2, COLS), BF16),
        ),
        in_specs=[anywhere] * 10,
        out_specs=(anywhere, pl.BlockSpec(memory_space=pltpu.VMEM)),
        scratch_shapes=[
            pltpu.VMEM((PAD, D), BF16),
            pltpu.VMEM((D, D), BF16),
            pltpu.VMEM((D,), F32),
            pltpu.VMEM((COLS, D), BF16),
            pltpu.VMEM((COLS, D), BF16),
            pltpu.VMEM((COLS, D), BF16),
            pltpu.VMEM((COLS, D), BF16),
            pltpu.VMEM((16, 128), jnp.int32),
            pltpu.VMEM((1, 256), jnp.int32),
            pltpu.VMEM((1, 256), jnp.int32),
            pltpu.VMEM((NZ, NG, D), BF16),
            pltpu.VMEM((NZ, NG, D), BF16),
            pltpu.VMEM((CHUNKS, 2, 2, 2 * CHUNK, D), BF16),
            pltpu.VMEM((2, NG, CHUNKS, 2 * CHUNK, D), BF16),
            pltpu.VMEM((SLOTS, SLOTS), BF16),
            pltpu.VMEM((2, COLS, SLOTS), BF16),
            pltpu.VMEM((NX, 8, 256), F32),
            pltpu.VMEM((NX - 1, 8, 256), F32),
            dma((10,)),
            dma,
            dma((NZ,)),
            dma((NZ,)),
            dma((CHUNKS, NX, 2)),
            dma((CHUNKS, NG)),
            dma((NX - 1,)),
            dma((NX - 1,)),
            dma((2,)),
        ],
        compiler_params=pltpu.CompilerParams(
            collective_id=0, has_side_effects=True, vmem_limit_bytes=60 * 1024 * 1024
        ),
        name="regroup_attend",
    )(
        tile_features, tile_weight, tile_bias, query_weight.T, key_weight.T, value_weight.T,
        output_weight, tile_region.reshape(TILE, 128), region_block.reshape(1, 256),
        region_count.reshape(1, 256),
    )
    return mixed.transpose(0, 2, 1), region


def solution(mesh):
    in_specs = (
        P("dp", None),
        P(),
        P(),
        P(None, "head"),
        P(None, "head"),
        P(None, "head"),
        P("head", None),
        P(),
        P(),
        P(),
    )
    out_specs = (P("dp", None, "head"), P("dp", "head"))
    return jax.shard_map(local, mesh=mesh, in_specs=in_specs, out_specs=out_specs, check_vma=False)
```

```python
import functools

import jax
import jax.numpy as jnp
from jax import lax
from jax.experimental import pallas as pl
from jax.experimental.pallas import tpu as pltpu
from jax.sharding import PartitionSpec as P

D = 768
SLOTS = 256
HD = 64
COLS = 192
TILE = 352
PAD = 384
NZ, NG, NX = 16, 8, 4
EMPTY = -8.0
MESH = pl.DeviceIdType.MESH
F32 = jnp.float32
BF16 = jnp.bfloat16
LAST = (((1,), (1,)), ((), ()))
CHUNK = 4
CHUNKS = NZ // CHUNK
OFFSETS = (0, 1, 15, 2, 14, 3, 13, 4, 12, 5, 11, 6, 10, 7, 9, 8)
ISSUE = (1, 15, 2, 14, 3, 13, 4, 12, 5, 11, 6, 10, 7, 9, 8)


def iota(shape, dim):
    return lax.broadcasted_iota(jnp.int32, shape, dim)


def kernel(
    feat, w, bias, wq, wk, wv, wo, reg, blk, cnt,
    mixed_out, region_out,
    f_v, w_v, bias_v, wq_v, wk_v, wv_v, wo_v, reg_v, blk_v, cnt_v,
    e_v, z_v, c_v, a_v, q_v, k_v, perm_v, s_v, r_v,
    in_sem, own_sem, zs_sem, zr_sem, xs_sem, xr_sem, ps_sem, pr_sem,
):
    dp = lax.axis_index("dp")
    h = lax.axis_index("head")
    z = dp // NG
    g = dp % NG
    y = g // 2
    core = g % 2

    first_row = (dp * TILE) // 128
    lane_off = (dp * TILE) % 128
    reg_base = pl.multiple_of(jnp.minimum((first_row // 8) * 8, TILE - 16), 8)
    loads = [
        pltpu.make_async_copy(reg.at[pl.ds(reg_base, 16)], reg_v, in_sem.at[0]),
        pltpu.make_async_copy(blk, blk_v, in_sem.at[1]),
        pltpu.make_async_copy(feat, f_v.at[pl.ds(0, TILE)], in_sem.at[2]),
        pltpu.make_async_copy(w, w_v, in_sem.at[3]),
        pltpu.make_async_copy(bias, bias_v, in_sem.at[4]),
        pltpu.make_async_copy(wq, wq_v, in_sem.at[5]),
        pltpu.make_async_copy(wk, wk_v, in_sem.at[6]),
        pltpu.make_async_copy(wv, wv_v, in_sem.at[7]),
        pltpu.make_async_copy(wo, wo_v, in_sem.at[8]),
        pltpu.make_async_copy(cnt, cnt_v, in_sem.at[9]),
    ]
    for load in loads:
        load.start()

    barrier = pltpu.get_barrier_semaphore()
    for o in range(NG):
        source = (g + o) % NG
        if o == 0:
            @pl.when(y != h)
            def _():
                pl.semaphore_signal(
                    barrier, inc=1, device_id={"dp": dp, "head": y}, device_id_type=MESH
                )
        else:
            pl.semaphore_signal(
                barrier, inc=1, device_id={"dp": z * NG + source, "head": y}, device_id_type=MESH
            )
    for o in range(1, NZ):
        pl.semaphore_signal(
            barrier, inc=1, device_id={"dp": ((z + o) % NZ) * NG + g, "head": h}, device_id_type=MESH
        )
    for o in range(1, NX):
        pl.semaphore_signal(
            barrier, inc=1, device_id={"dp": dp, "head": (h + o) % NX}, device_id_type=MESH
        )

    f_v[pl.ds(TILE, PAD - TILE), :] = jnp.zeros((PAD - TILE, D), BF16)
    upper = (iota((PAD, PAD), 0) < iota((PAD, PAD), 1)).astype(F32).astype(BF16)
    loads[0].wait()
    loads[1].wait()
    parts = []
    for i in range(4):
        at = jnp.minimum(first_row + i, TILE - 1) - reg_base
        parts.append(reg_v[pl.ds(at, 1), :])
    line = jnp.broadcast_to(jnp.concatenate(parts, axis=1), (8, 512))
    line = pltpu.roll(line, (512 - lane_off) % 512, 1)[:, :PAD]
    in_range = iota((8, PAD), 1) < TILE
    line = jnp.where(in_range, line, -1)
    hot = (iota((256, PAD), 0) == line[0:1, :]).astype(F32)
    hot16 = hot.astype(BF16)
    block_row = jnp.broadcast_to(blk_v[...].astype(F32), (8, 256)).astype(BF16)
    block = jnp.dot(block_row, hot16, preferred_element_type=F32)
    before = jnp.dot(hot16, upper, preferred_element_type=F32)
    rank = jnp.sum(before * hot, axis=0, keepdims=True)
    code = jnp.where(in_range[0:1, :], block[0:1, :] * 2.0 + rank, -1.0)
    row = iota((128, PAD), 0)
    target = (32 * (row // NG) + 8 * h + row % NG).astype(F32)
    pick = (code == target).astype(F32)
    live = jnp.sum(pick, axis=1, keepdims=True)
    loads[2].wait()
    x = jnp.dot(pick.astype(BF16), f_v[...], preferred_element_type=F32).astype(BF16)
    loads[3].wait()
    loads[4].wait()
    hidden = jnp.dot(x, w_v[...], preferred_element_type=F32) + bias_v[...].reshape(1, D)
    embedded = jax.nn.gelu(hidden, approximate=True)
    embedded = jnp.where(live > 0.5, embedded, EMPTY).astype(BF16)
    e_v[...] = embedded.reshape(NZ, NG, D)

    pl.semaphore_wait(barrier, NG + NZ - 1 + NX - 1 - (y == h).astype(jnp.int32))

    z_sends = {}
    for offset in ISSUE:
        p = OFFSETS.index(offset)
        to = (z + NZ - offset) % NZ
        copy = pltpu.make_async_remote_copy(
            src_ref=e_v.at[to],
            dst_ref=z_v.at[p],
            send_sem=zs_sem.at[p],
            recv_sem=zr_sem.at[p],
            device_id={"dp": to * NG + g, "head": h},
            device_id_type=MESH,
        )
        copy.start()
        z_sends[p] = copy
    own = pltpu.make_async_copy(e_v.at[z], z_v.at[0], own_sem)
    own.start()

    at = iota((SLOTS, SLOTS), 0)
    slot = iota((SLOTS, SLOTS), 1)
    place = (at // 64) * CHUNK + at % CHUNK
    off = jnp.zeros((SLOTS, SLOTS), jnp.int32)
    for p in range(1, NZ):
        off = jnp.where(place == p, OFFSETS[p], off)
    to_slot = (((z + off) % NZ) * NG + at // 8 % NG) * 2 + at // CHUNK % 2
    perm_v[...] = (slot == to_slot).astype(F32).astype(BF16)

    rows = 8 * CHUNK
    out_row = iota((rows, rows), 0)
    in_row = (out_row % CHUNK) * 8 + out_row // 8 % 2 * 2 + out_row // 16 * 4 + out_row // CHUNK % 2
    order = (iota((rows, rows), 1) == in_row).astype(F32).astype(BF16)
    x_sends = []
    local_sends = []
    for n in range(CHUNKS):
        for p in range(n * CHUNK, (n + 1) * CHUNK):
            if p == 0:
                own.wait()
            else:
                z_sends[p].wait_recv()
        arrived = z_v[n * CHUNK : (n + 1) * CHUNK].reshape(rows, D)
        turned = jnp.dot(order, arrived, preferred_element_type=F32).astype(BF16)
        c_v[n] = turned.reshape(2, 2, 2 * CHUNK, D)
        for o in (2, 1, 3, 0):
            for oc in (1, 0):
                to = (h + o) % NX
                to_core = (core + oc) % 2
                copy = pltpu.make_async_remote_copy(
                    src_ref=c_v.at[n, to_core],
                    dst_ref=a_v.at[:, n, g],
                    send_sem=xs_sem.at[n, o, oc],
                    recv_sem=xr_sem.at[n, g],
                    device_id={"dp": z * NG + h * 2 + to_core, "head": to},
                    device_id_type=MESH,
                )
                if o == 0 and oc == 0:
                    here = pltpu.make_async_copy(
                        c_v.at[n, to_core], a_v.at[:, n, g], xr_sem.at[n, g]
                    )
                    pl.when(y == h)(here.start)
                    pl.when(y != h)(copy.start)
                    local_sends.append(copy)
                else:
                    copy.start()
                    x_sends.append(copy)

    for load in loads[5:]:
        load.wait()
    counts = []
    for j in range(2):
        here = blk_v[...] == dp * 2 + j
        counts.append(
            jnp.sum(jnp.where(here, cnt_v[...].astype(F32), 0.0), axis=1, keepdims=True)
        )
    size = 16 * CHUNK
    for n in range(CHUNKS):
        for source in range(NG):
            landed = a_v.at[:, n, source]
            pltpu.make_async_copy(landed, landed, xr_sem.at[n, source]).wait()
        rows = a_v[:, n].reshape(2 * size, D)
        for weight, kept in ((wk_v, k_v), (wq_v, q_v)):
            made = lax.dot_general(rows, weight[...], LAST, preferred_element_type=F32)
            kept[:, n * size : (n + 1) * size] = made.astype(BF16).reshape(2, size, COLS)

    lane = iota((SLOTS, COLS), 1)
    first = (iota((8, 128), 1) == 0).astype(F32).astype(BF16)
    pairs = [(j, n) for j in range(2) for n in range(3)]
    alive, alive_row, scores, vals = [], [], {}, []
    for j in range(2):
        marks = a_v[j, :, :, :, 0:128].reshape(SLOTS, 128)
        alive.append(marks[:, 0:1].astype(F32) > -4.0)
        mark = lax.dot_general(first, marks, LAST, preferred_element_type=F32)
        alive_row.append((mark > -4.0).astype(F32).astype(BF16))
    for j, n in pairs:
        keys = k_v[j]
        mine = (lane >= n * HD) & (lane < (n + 1) * HD)
        head_keys = jnp.where(mine, keys, jnp.zeros_like(keys))
        scores[j, n] = lax.dot_general(head_keys, q_v[j], LAST, preferred_element_type=F32)
    for j in range(2):
        rows = a_v[j].reshape(SLOTS, D)
        made = lax.dot_general(wv_v[...], rows, LAST, preferred_element_type=F32)
        vals.append(made.astype(BF16))
    parts = {}
    for j, n in pairs:
        masked = scores[j, n] * (HD ** -0.5) + jnp.where(alive[j], 0.0, -1e30)
        top = jnp.max(masked, axis=0, keepdims=True)
        weights = jnp.exp(masked - top)
        inverse = 1.0 / jnp.sum(weights, axis=0, keepdims=True)
        part = jnp.dot(
            vals[j][n * HD : (n + 1) * HD], weights.astype(BF16), preferred_element_type=F32
        )
        parts[j, n] = (part * inverse).astype(BF16)
    mixed = [jnp.concatenate([parts[j, n] for n in range(3)], axis=0) for j in range(2)]
    pooled = jnp.zeros((8, COLS), F32)
    for j in range(2):
        total = lax.dot_general(alive_row[j], mixed[j], LAST, preferred_element_type=F32)
        pooled = jnp.where(iota((8, COLS), 0) == j, total / counts[j], pooled)
    partial = jnp.dot(pooled.astype(BF16), wo_v[...], preferred_element_type=F32)
    for i in range(NX):
        s_v[i, :, 0:COLS] = partial[:, i * COLS : (i + 1) * COLS]
        s_v[i, :, COLS:256] = jnp.zeros((8, 256 - COLS), F32)
    p_sends = []
    for o in range(1, NX):
        to = (h + o) % NX
        copy = pltpu.make_async_remote_copy(
            src_ref=s_v.at[to],
            dst_ref=r_v.at[o - 1],
            send_sem=ps_sem.at[o - 1],
            recv_sem=pr_sem.at[o - 1],
            device_id={"dp": dp, "head": to},
            device_id_type=MESH,
        )
        copy.start()
        p_sends.append(copy)
    for j in range(2):
        ordered = jnp.where(alive[j], perm_v[...].astype(F32), 0.0).astype(BF16)
        result = jnp.dot(mixed[j], ordered, preferred_element_type=F32)
        mixed_out[j] = result.astype(BF16)
    for copy in z_sends.values():
        copy.wait_send()
    for copy in x_sends:
        copy.wait_send()
    for copy in local_sends:
        pl.when(y != h)(copy.wait_send)
    own_part = s_v[h]
    for copy in p_sends:
        copy.wait_recv()
    everything = own_part + r_v[0] + r_v[1] + r_v[2]
    region_out[...] = everything[0:2, 0:COLS].astype(BF16)
    for copy in p_sends:
        copy.wait_send()


def local(
    tile_features, tile_weight, tile_bias, query_weight, key_weight, value_weight, output_weight,
    tile_region, region_block, region_count,
):
    dma = pltpu.SemaphoreType.DMA
    anywhere = pl.BlockSpec(memory_space=pl.ANY)
    mixed, region = pl.pallas_call(
        kernel,
        out_shape=(
            pltpu.VMEM((2, COLS, SLOTS), BF16),
            pltpu.VMEM((2, COLS), BF16),
        ),
        in_specs=[anywhere] * 10,
        out_specs=(pl.BlockSpec(memory_space=pltpu.VMEM), pl.BlockSpec(memory_space=pltpu.VMEM)),
        scratch_shapes=[
            pltpu.VMEM((PAD, D), BF16),
            pltpu.VMEM((D, D), BF16),
            pltpu.VMEM((D,), F32),
            pltpu.VMEM((COLS, D), BF16),
            pltpu.VMEM((COLS, D), BF16),
            pltpu.VMEM((COLS, D), BF16),
            pltpu.VMEM((COLS, D), BF16),
            pltpu.VMEM((16, 128), jnp.int32),
            pltpu.VMEM((1, 256), jnp.int32),
            pltpu.VMEM((1, 256), jnp.int32),
            pltpu.VMEM((NZ, NG, D), BF16),
            pltpu.VMEM((NZ, NG, D), BF16),
            pltpu.VMEM((CHUNKS, 2, 2, 2 * CHUNK, D), BF16),
            pltpu.VMEM((2, CHUNKS, NG, 2 * CHUNK, D), BF16),
            pltpu.VMEM((2, SLOTS, COLS), BF16),
            pltpu.VMEM((2, SLOTS, COLS), BF16),
            pltpu.VMEM((SLOTS, SLOTS), BF16),
            pltpu.VMEM((NX, 8, 256), F32),
            pltpu.VMEM((NX - 1, 8, 256), F32),
            dma((10,)),
            dma,
            dma((NZ,)),
            dma((NZ,)),
            dma((CHUNKS, NX, 2)),
            dma((CHUNKS, NG)),
            dma((NX - 1,)),
            dma((NX - 1,)),
        ],
        compiler_params=pltpu.CompilerParams(
            collective_id=0, has_side_effects=True, vmem_limit_bytes=60 * 1024 * 1024
        ),
        name="regroup_attend",
    )(
        tile_features, tile_weight, tile_bias, query_weight.T, key_weight.T, value_weight.T,
        output_weight, tile_region.reshape(TILE, 128), region_block.reshape(1, 256),
        region_count.reshape(1, 256),
    )
    return mixed.transpose(0, 2, 1), region


def solution(mesh):
    in_specs = (
        P("dp", None),
        P(),
        P(),
        P(None, "head"),
        P(None, "head"),
        P(None, "head"),
        P("head", None),
        P(),
        P(),
        P(),
    )
    out_specs = (P("dp", None, "head"), P("dp", "head"))
    return jax.shard_map(local, mesh=mesh, in_specs=in_specs, out_specs=out_specs, check_vma=False)
```

```python
import functools

import jax
import jax.numpy as jnp
from jax import lax
from jax.experimental import pallas as pl
from jax.experimental.pallas import tpu as pltpu
from jax.sharding import PartitionSpec as P

D = 768
SLOTS = 256
HD = 64
COLS = 192
TILE = 352
PAD = 384
NZ, NG, NX = 16, 8, 4
EMPTY = -8.0
MESH = pl.DeviceIdType.MESH
F32 = jnp.float32
BF16 = jnp.bfloat16
LAST = (((1,), (1,)), ((), ()))
CHUNK = 4
CHUNKS = NZ // CHUNK
OFFSETS = (0, 1, 15, 2, 14, 3, 13, 4, 12, 5, 11, 6, 10, 7, 9, 8)
ISSUE = (1, 15, 2, 14, 3, 13, 4, 12, 5, 11, 6, 10, 7, 9, 8)


def iota(shape, dim):
    return lax.broadcasted_iota(jnp.int32, shape, dim)


def kernel(
    feat, w, bias, wq, wk, wv, wo, reg, blk, cnt,
    mixed_out, region_out,
    f_v, w_v, bias_v, wq_v, wk_v, wv_v, wo_v, reg_v, blk_v, cnt_v,
    e_v, z_v, c_v, a_v, q_v, k_v, perm_v, s_v, r_v,
    in_sem, own_sem, zs_sem, zr_sem, xs_sem, xr_sem, ps_sem, pr_sem,
):
    dp = lax.axis_index("dp")
    h = lax.axis_index("head")
    z = dp // NG
    g = dp % NG
    y = g // 2
    core = g % 2

    first_row = (dp * TILE) // 128
    lane_off = (dp * TILE) % 128
    reg_base = pl.multiple_of(jnp.minimum((first_row // 8) * 8, TILE - 16), 8)
    loads = [
        pltpu.make_async_copy(reg.at[pl.ds(reg_base, 16)], reg_v, in_sem.at[0]),
        pltpu.make_async_copy(blk, blk_v, in_sem.at[1]),
        pltpu.make_async_copy(feat, f_v.at[pl.ds(0, TILE)], in_sem.at[2]),
        pltpu.make_async_copy(w, w_v, in_sem.at[3]),
        pltpu.make_async_copy(bias, bias_v, in_sem.at[4]),
        pltpu.make_async_copy(wq, wq_v, in_sem.at[5]),
        pltpu.make_async_copy(wk, wk_v, in_sem.at[6]),
        pltpu.make_async_copy(wv, wv_v, in_sem.at[7]),
        pltpu.make_async_copy(wo, wo_v, in_sem.at[8]),
        pltpu.make_async_copy(cnt, cnt_v, in_sem.at[9]),
    ]
    barrier = pltpu.get_barrier_semaphore()
    for o in (8, 7, 9, 6, 10, 5, 11, 4, 12, 3, 13, 2, 14, 1, 15):
        pl.semaphore_signal(
            barrier, inc=1, device_id={"dp": ((z + o) % NZ) * NG + g, "head": h}, device_id_type=MESH
        )
    for o in range(NG):
        source = (g + o) % NG
        if o == 0:
            @pl.when(y != h)
            def _():
                pl.semaphore_signal(
                    barrier, inc=1, device_id={"dp": dp, "head": y}, device_id_type=MESH
                )
        else:
            pl.semaphore_signal(
                barrier, inc=1, device_id={"dp": z * NG + source, "head": y}, device_id_type=MESH
            )
    for o in range(1, NX):
        pl.semaphore_signal(
            barrier, inc=1, device_id={"dp": dp, "head": (h + o) % NX}, device_id_type=MESH
        )
    for load in loads:
        load.start()

    f_v[pl.ds(TILE, PAD - TILE), :] = jnp.zeros((PAD - TILE, D), BF16)
    upper = (iota((PAD, PAD), 0) < iota((PAD, PAD), 1)).astype(F32).astype(BF16)
    loads[0].wait()
    loads[1].wait()
    parts = []
    for i in range(4):
        at = jnp.minimum(first_row + i, TILE - 1) - reg_base
        parts.append(reg_v[pl.ds(at, 1), :])
    line = jnp.broadcast_to(jnp.concatenate(parts, axis=1), (8, 512))
    line = pltpu.roll(line, (512 - lane_off) % 512, 1)[:, :PAD]
    in_range = iota((8, PAD), 1) < TILE
    line = jnp.where(in_range, line, -1)
    hot = (iota((256, PAD), 0) == line[0:1, :]).astype(F32)
    hot16 = hot.astype(BF16)
    block_row = jnp.broadcast_to(blk_v[...].astype(F32), (8, 256)).astype(BF16)
    block = jnp.dot(block_row, hot16, preferred_element_type=F32)
    before = jnp.dot(hot16, upper, preferred_element_type=F32)
    rank = jnp.sum(before * hot, axis=0, keepdims=True)
    code = jnp.where(in_range[0:1, :], block[0:1, :] * 2.0 + rank, -1.0)
    row = iota((128, PAD), 0)
    target = (32 * (row // NG) + 8 * h + row % NG).astype(F32)
    pick = (code == target).astype(F32)
    live = jnp.sum(pick, axis=1, keepdims=True)
    loads[2].wait()
    x = jnp.dot(pick.astype(BF16), f_v[...], preferred_element_type=F32).astype(BF16)
    loads[3].wait()
    loads[4].wait()
    hidden = jnp.dot(x, w_v[...], preferred_element_type=F32) + bias_v[...].reshape(1, D)
    embedded = jax.nn.gelu(hidden, approximate=True)
    embedded = jnp.where(live > 0.5, embedded, EMPTY).astype(BF16)
    e_v[...] = embedded.reshape(NZ, NG, D)

    pl.semaphore_wait(barrier, NG + NZ - 1 + NX - 1 - (y == h).astype(jnp.int32))

    z_sends = {}
    for offset in ISSUE:
        p = OFFSETS.index(offset)
        to = (z + NZ - offset) % NZ
        copy = pltpu.make_async_remote_copy(
            src_ref=e_v.at[to],
            dst_ref=z_v.at[p],
            send_sem=zs_sem.at[p],
            recv_sem=zr_sem.at[p],
            device_id={"dp": to * NG + g, "head": h},
            device_id_type=MESH,
        )
        copy.start()
        z_sends[p] = copy
    own = pltpu.make_async_copy(e_v.at[z], z_v.at[0], own_sem)
    own.start()

    at = iota((SLOTS, SLOTS), 0)
    slot = iota((SLOTS, SLOTS), 1)
    place = (at // 64) * CHUNK + at % CHUNK
    off = jnp.zeros((SLOTS, SLOTS), jnp.int32)
    for p in range(1, NZ):
        off = jnp.where(place == p, OFFSETS[p], off)
    to_slot = (((z + off) % NZ) * NG + at // 8 % NG) * 2 + at // CHUNK % 2
    perm_v[...] = (slot == to_slot).astype(F32).astype(BF16)

    rows = 8 * CHUNK
    out_row = iota((rows, rows), 0)
    in_row = (out_row % CHUNK) * 8 + out_row // 8 % 2 * 2 + out_row // 16 * 4 + out_row // CHUNK % 2
    order = (iota((rows, rows), 1) == in_row).astype(F32).astype(BF16)
    x_sends = []
    local_sends = []
    for n in range(CHUNKS):
        for p in range(n * CHUNK, (n + 1) * CHUNK):
            if p == 0:
                own.wait()
            else:
                z_sends[p].wait_recv()
        arrived = z_v[n * CHUNK : (n + 1) * CHUNK].reshape(rows, D)
        turned = jnp.dot(order, arrived, preferred_element_type=F32).astype(BF16)
        c_v[n] = turned.reshape(2, 2, 2 * CHUNK, D)
        for o in (2, 1, 3, 0):
            for oc in (1, 0):
                to = (h + o) % NX
                to_core = (core + oc) % 2
                copy = pltpu.make_async_remote_copy(
                    src_ref=c_v.at[n, to_core],
                    dst_ref=a_v.at[:, n, g],
                    send_sem=xs_sem.at[n, o, oc],
                    recv_sem=xr_sem.at[n, g],
                    device_id={"dp": z * NG + h * 2 + to_core, "head": to},
                    device_id_type=MESH,
                )
                if o == 0 and oc == 0:
                    here = pltpu.make_async_copy(
                        c_v.at[n, to_core], a_v.at[:, n, g], xr_sem.at[n, g]
                    )
                    pl.when(y == h)(here.start)
                    pl.when(y != h)(copy.start)
                    local_sends.append(copy)
                else:
                    copy.start()
                    x_sends.append(copy)

    for load in loads[5:]:
        load.wait()
    counts = []
    for j in range(2):
        here = blk_v[...] == dp * 2 + j
        counts.append(
            jnp.sum(jnp.where(here, cnt_v[...].astype(F32), 0.0), axis=1, keepdims=True)
        )
    size = 16 * CHUNK
    for n in range(CHUNKS):
        if n == CHUNKS - 1:
            for copy in z_sends.values():
                copy.wait_send()
            for copy in x_sends[:-7]:
                copy.wait_send()
            for copy in local_sends[:-1]:
                pl.when(y != h)(copy.wait_send)
        for source in range(NG):
            landed = a_v.at[:, n, source]
            pltpu.make_async_copy(landed, landed, xr_sem.at[n, source]).wait()
        rows = a_v[:, n].reshape(2 * size, D)
        for weight, kept in ((wk_v, k_v), (wq_v, q_v)):
            made = lax.dot_general(rows, weight[...], LAST, preferred_element_type=F32)
            kept[:, n * size : (n + 1) * size] = made.astype(BF16).reshape(2, size, COLS)

    lane = iota((SLOTS, COLS), 1)
    first = (iota((8, 128), 1) == 0).astype(F32).astype(BF16)
    pairs = [(j, n) for j in range(2) for n in range(3)]
    alive, alive_row, scores, vals = [], [], {}, []
    for j in range(2):
        marks = a_v[j, :, :, :, 0:128].reshape(SLOTS, 128)
        alive.append(marks[:, 0:1].astype(F32) > -4.0)
        mark = lax.dot_general(first, marks, LAST, preferred_element_type=F32)
        alive_row.append((mark > -4.0).astype(F32).astype(BF16))
    for j, n in pairs:
        keys = k_v[j]
        mine = (lane >= n * HD) & (lane < (n + 1) * HD)
        head_keys = jnp.where(mine, keys, jnp.zeros_like(keys))
        scores[j, n] = lax.dot_general(head_keys, q_v[j], LAST, preferred_element_type=F32)
    for j in range(2):
        rows = a_v[j].reshape(SLOTS, D)
        made = lax.dot_general(wv_v[...], rows, LAST, preferred_element_type=F32)
        vals.append(made.astype(BF16))
    parts = {}
    for j, n in pairs:
        masked = scores[j, n] * (HD ** -0.5) + jnp.where(alive[j], 0.0, -1e30)
        top = jnp.max(masked, axis=0, keepdims=True)
        weights = jnp.exp(masked - top)
        inverse = 1.0 / jnp.sum(weights, axis=0, keepdims=True)
        part = jnp.dot(
            vals[j][n * HD : (n + 1) * HD], weights.astype(BF16), preferred_element_type=F32
        )
        parts[j, n] = (part * inverse).astype(BF16)
    mixed = [jnp.concatenate([parts[j, n] for n in range(3)], axis=0) for j in range(2)]
    pooled = jnp.zeros((8, COLS), F32)
    for j in range(2):
        total = lax.dot_general(alive_row[j], mixed[j], LAST, preferred_element_type=F32)
        pooled = jnp.where(iota((8, COLS), 0) == j, total / counts[j], pooled)
    partial = jnp.dot(pooled.astype(BF16), wo_v[...], preferred_element_type=F32)
    for i in range(NX):
        s_v[i, :, 0:COLS] = partial[:, i * COLS : (i + 1) * COLS]
        s_v[i, :, COLS:256] = jnp.zeros((8, 256 - COLS), F32)
    p_sends = []
    for o in range(1, NX):
        to = (h + o) % NX
        copy = pltpu.make_async_remote_copy(
            src_ref=s_v.at[to],
            dst_ref=r_v.at[o - 1],
            send_sem=ps_sem.at[o - 1],
            recv_sem=pr_sem.at[o - 1],
            device_id={"dp": dp, "head": to},
            device_id_type=MESH,
        )
        copy.start()
        p_sends.append(copy)
    for j in range(2):
        ordered = jnp.where(alive[j], perm_v[...].astype(F32), 0.0).astype(BF16)
        result = jnp.dot(mixed[j], ordered, preferred_element_type=F32)
        mixed_out[j] = result.astype(BF16)
    for copy in x_sends[-7:]:
        copy.wait_send()
    pl.when(y != h)(local_sends[-1].wait_send)
    own_part = s_v[h]
    for copy in p_sends:
        copy.wait_recv()
    everything = own_part + r_v[0] + r_v[1] + r_v[2]
    region_out[...] = everything[0:2, 0:COLS].astype(BF16)
    for copy in p_sends:
        copy.wait_send()


def local(
    tile_features, tile_weight, tile_bias, query_weight, key_weight, value_weight, output_weight,
    tile_region, region_block, region_count,
):
    dma = pltpu.SemaphoreType.DMA
    anywhere = pl.BlockSpec(memory_space=pl.ANY)
    mixed, region = pl.pallas_call(
        kernel,
        out_shape=(
            pltpu.VMEM((2, COLS, SLOTS), BF16),
            pltpu.VMEM((2, COLS), BF16),
        ),
        in_specs=[anywhere] * 10,
        out_specs=(pl.BlockSpec(memory_space=pltpu.VMEM), pl.BlockSpec(memory_space=pltpu.VMEM)),
        scratch_shapes=[
            pltpu.VMEM((PAD, D), BF16),
            pltpu.VMEM((D, D), BF16),
            pltpu.VMEM((D,), F32),
            pltpu.VMEM((COLS, D), BF16),
            pltpu.VMEM((COLS, D), BF16),
            pltpu.VMEM((COLS, D), BF16),
            pltpu.VMEM((COLS, D), BF16),
            pltpu.VMEM((16, 128), jnp.int32),
            pltpu.VMEM((1, 256), jnp.int32),
            pltpu.VMEM((1, 256), jnp.int32),
            pltpu.VMEM((NZ, NG, D), BF16),
            pltpu.VMEM((NZ, NG, D), BF16),
            pltpu.VMEM((CHUNKS, 2, 2, 2 * CHUNK, D), BF16),
            pltpu.VMEM((2, CHUNKS, NG, 2 * CHUNK, D), BF16),
            pltpu.VMEM((2, SLOTS, COLS), BF16),
            pltpu.VMEM((2, SLOTS, COLS), BF16),
            pltpu.VMEM((SLOTS, SLOTS), BF16),
            pltpu.VMEM((NX, 8, 256), F32),
            pltpu.VMEM((NX - 1, 8, 256), F32),
            dma((10,)),
            dma,
            dma((NZ,)),
            dma((NZ,)),
            dma((CHUNKS, NX, 2)),
            dma((CHUNKS, NG)),
            dma((NX - 1,)),
            dma((NX - 1,)),
        ],
        compiler_params=pltpu.CompilerParams(
            collective_id=0, has_side_effects=True, vmem_limit_bytes=60 * 1024 * 1024
        ),
        name="regroup_attend",
    )(
        tile_features, tile_weight, tile_bias, query_weight.T, key_weight.T, value_weight.T,
        output_weight, tile_region.reshape(TILE, 128), region_block.reshape(1, 256),
        region_count.reshape(1, 256),
    )
    return mixed.transpose(0, 2, 1), region


def solution(mesh):
    in_specs = (
        P("dp", None),
        P(),
        P(),
        P(None, "head"),
        P(None, "head"),
        P(None, "head"),
        P("head", None),
        P(),
        P(),
        P(),
    )
    out_specs = (P("dp", None, "head"), P("dp", "head"))
    return jax.shard_map(local, mesh=mesh, in_specs=in_specs, out_specs=out_specs, check_vma=False)
```

```python
import functools

import jax
import jax.numpy as jnp
from jax import lax
from jax.experimental import pallas as pl
from jax.experimental.pallas import tpu as pltpu
from jax.sharding import PartitionSpec as P

D = 768
SLOTS = 256
HD = 64
COLS = 192
TILE = 352
PAD = 384
NZ, NG, NX = 16, 8, 4
EMPTY = -8.0
MESH = pl.DeviceIdType.MESH
F32 = jnp.float32
BF16 = jnp.bfloat16
LAST = (((1,), (1,)), ((), ()))
CHUNK = 4
CHUNKS = NZ // CHUNK
OFFSETS = (0, 1, 15, 2, 14, 3, 13, 4, 12, 5, 11, 6, 10, 7, 9, 8)
DIRECT = (1, 15, 2, 14, 3, 13, 4, 12, 5, 11, 6, 10)


def iota(shape, dim):
    return lax.broadcasted_iota(jnp.int32, shape, dim)


def kernel(
    feat, w, bias, wq, wk, wv, wo, reg, blk, cnt,
    mixed_out, region_out,
    f_v, w_v, bias_v, wq_v, wk_v, wv_v, wo_v, reg_v, blk_v, cnt_v,
    e_v, z_v, up_v, down_v, c_v, a_v, q_v, k_v, perm_v, s_v, r_v,
    in_sem, own_sem, zs_sem, zr_sem, relay_sem, xs_sem, xr_sem, ps_sem, pr_sem,
):
    dp = lax.axis_index("dp")
    h = lax.axis_index("head")
    z = dp // NG
    g = dp % NG
    y = g // 2
    core = g % 2

    first_row = (dp * TILE) // 128
    lane_off = (dp * TILE) % 128
    reg_base = pl.multiple_of(jnp.minimum((first_row // 8) * 8, TILE - 16), 8)
    loads = [
        pltpu.make_async_copy(reg.at[pl.ds(reg_base, 16)], reg_v, in_sem.at[0]),
        pltpu.make_async_copy(blk, blk_v, in_sem.at[1]),
        pltpu.make_async_copy(feat, f_v.at[pl.ds(0, TILE)], in_sem.at[2]),
        pltpu.make_async_copy(w, w_v, in_sem.at[3]),
        pltpu.make_async_copy(bias, bias_v, in_sem.at[4]),
        pltpu.make_async_copy(wq, wq_v, in_sem.at[5]),
        pltpu.make_async_copy(wk, wk_v, in_sem.at[6]),
        pltpu.make_async_copy(wv, wv_v, in_sem.at[7]),
        pltpu.make_async_copy(wo, wo_v, in_sem.at[8]),
        pltpu.make_async_copy(cnt, cnt_v, in_sem.at[9]),
    ]
    barrier = pltpu.get_barrier_semaphore()
    for o in reversed(DIRECT):
        pl.semaphore_signal(
            barrier, inc=1, device_id={"dp": ((z + o) % NZ) * NG + g, "head": h}, device_id_type=MESH
        )
    for o in range(NG):
        source = (g + o) % NG
        if o == 0:
            @pl.when(y != h)
            def _():
                pl.semaphore_signal(
                    barrier, inc=1, device_id={"dp": dp, "head": y}, device_id_type=MESH
                )
        else:
            pl.semaphore_signal(
                barrier, inc=1, device_id={"dp": z * NG + source, "head": y}, device_id_type=MESH
            )
    for o in range(1, NX):
        pl.semaphore_signal(
            barrier, inc=1, device_id={"dp": dp, "head": (h + o) % NX}, device_id_type=MESH
        )
    for load in loads:
        load.start()

    f_v[pl.ds(TILE, PAD - TILE), :] = jnp.zeros((PAD - TILE, D), BF16)
    upper = (iota((PAD, PAD), 0) < iota((PAD, PAD), 1)).astype(F32).astype(BF16)
    loads[0].wait()
    loads[1].wait()
    parts = []
    for i in range(4):
        at = jnp.minimum(first_row + i, TILE - 1) - reg_base
        parts.append(reg_v[pl.ds(at, 1), :])
    line = jnp.broadcast_to(jnp.concatenate(parts, axis=1), (8, 512))
    line = pltpu.roll(line, (512 - lane_off) % 512, 1)[:, :PAD]
    in_range = iota((8, PAD), 1) < TILE
    line = jnp.where(in_range, line, -1)
    hot = (iota((256, PAD), 0) == line[0:1, :]).astype(F32)
    hot16 = hot.astype(BF16)
    block_row = jnp.broadcast_to(blk_v[...].astype(F32), (8, 256)).astype(BF16)
    block = jnp.dot(block_row, hot16, preferred_element_type=F32)
    before = jnp.dot(hot16, upper, preferred_element_type=F32)
    rank = jnp.sum(before * hot, axis=0, keepdims=True)
    code = jnp.where(in_range[0:1, :], block[0:1, :] * 2.0 + rank, -1.0)
    row = iota((128, PAD), 0)
    target = (32 * ((z + row // NG) % NZ) + 8 * h + row % NG).astype(F32)
    pick = (code == target).astype(F32)
    live = jnp.sum(pick, axis=1, keepdims=True)
    loads[2].wait()
    x = jnp.dot(pick.astype(BF16), f_v[...], preferred_element_type=F32).astype(BF16)
    loads[3].wait()
    loads[4].wait()
    hidden = jnp.dot(x, w_v[...], preferred_element_type=F32) + bias_v[...].reshape(1, D)
    embedded = jax.nn.gelu(hidden, approximate=True)
    embedded = jnp.where(live > 0.5, embedded, EMPTY).astype(BF16)
    e_v[...] = embedded.reshape(NZ, NG, D)

    pl.semaphore_wait(barrier, NG + len(DIRECT) + NX - 1 - (y == h).astype(jnp.int32))

    def along_z(source, target, away, sent, got):
        copy = pltpu.make_async_remote_copy(
            src_ref=source,
            dst_ref=target,
            send_sem=zs_sem.at[sent],
            recv_sem=got,
            device_id={"dp": ((z + away) % NZ) * NG + g, "head": h},
            device_id_type=MESH,
        )
        copy.start()
        return copy

    up = along_z(e_v.at[pl.ds(7, 2)], up_v, 3, 0, relay_sem.at[0])
    down = along_z(e_v.at[pl.ds(9, 1)], down_v, 13, NZ, relay_sem.at[1])
    z_sends = {}
    for k in DIRECT:
        p = OFFSETS.index(NZ - k)
        z_sends[p] = along_z(e_v.at[k], z_v.at[p], k, p, zr_sem.at[p])
    own = pltpu.make_async_copy(e_v.at[0], z_v.at[0], own_sem)
    own.start()

    at = iota((SLOTS, SLOTS), 0)
    slot = iota((SLOTS, SLOTS), 1)
    place = (at // 64) * CHUNK + at % CHUNK
    off = jnp.zeros((SLOTS, SLOTS), jnp.int32)
    for p in range(1, NZ):
        off = jnp.where(place == p, OFFSETS[p], off)
    to_slot = (((z + off) % NZ) * NG + at // 8 % NG) * 2 + at // CHUNK % 2
    perm_v[...] = (slot == to_slot).astype(F32).astype(BF16)

    rows = 8 * CHUNK
    out_row = iota((rows, rows), 0)
    in_row = (out_row % CHUNK) * 8 + out_row // 8 % 2 * 2 + out_row // 16 * 4 + out_row // CHUNK % 2
    order = (iota((rows, rows), 1) == in_row).astype(F32).astype(BF16)
    up.wait_recv()
    down.wait_recv()
    for source, away, offset in ((up_v.at[1], 5, 8), (up_v.at[0], 4, 9), (down_v.at[0], 12, 7)):
        p = OFFSETS.index(offset)
        z_sends[p] = along_z(source, z_v.at[p], away, p, zr_sem.at[p])

    x_sends = []
    local_sends = []
    for n in range(CHUNKS):
        for p in range(n * CHUNK, (n + 1) * CHUNK):
            if p == 0:
                own.wait()
            else:
                z_sends[p].wait_recv()
        arrived = z_v[n * CHUNK : (n + 1) * CHUNK].reshape(rows, D)
        turned = jnp.dot(order, arrived, preferred_element_type=F32).astype(BF16)
        c_v[n] = turned.reshape(2, 2, 2 * CHUNK, D)
        for o in (2, 1, 3, 0):
            for oc in (1, 0):
                to = (h + o) % NX
                to_core = (core + oc) % 2
                copy = pltpu.make_async_remote_copy(
                    src_ref=c_v.at[n, to_core],
                    dst_ref=a_v.at[:, n, g],
                    send_sem=xs_sem.at[n, o, oc],
                    recv_sem=xr_sem.at[n, g],
                    device_id={"dp": z * NG + h * 2 + to_core, "head": to},
                    device_id_type=MESH,
                )
                if o == 0 and oc == 0:
                    here = pltpu.make_async_copy(
                        c_v.at[n, to_core], a_v.at[:, n, g], xr_sem.at[n, g]
                    )
                    pl.when(y == h)(here.start)
                    pl.when(y != h)(copy.start)
                    local_sends.append(copy)
                else:
                    copy.start()
                    x_sends.append(copy)

    for load in loads[5:]:
        load.wait()
    counts = []
    for j in range(2):
        here = blk_v[...] == dp * 2 + j
        counts.append(
            jnp.sum(jnp.where(here, cnt_v[...].astype(F32), 0.0), axis=1, keepdims=True)
        )
    size = 16 * CHUNK
    for n in range(CHUNKS):
        if n == CHUNKS - 1:
            for copy in (up, down, *z_sends.values()):
                copy.wait_send()
            for copy in x_sends[:-7]:
                copy.wait_send()
            for copy in local_sends[:-1]:
                pl.when(y != h)(copy.wait_send)
        for source in range(NG):
            landed = a_v.at[:, n, source]
            pltpu.make_async_copy(landed, landed, xr_sem.at[n, source]).wait()
        rows = a_v[:, n].reshape(2 * size, D)
        for weight, kept in ((wk_v, k_v), (wq_v, q_v)):
            made = lax.dot_general(rows, weight[...], LAST, preferred_element_type=F32)
            kept[:, n * size : (n + 1) * size] = made.astype(BF16).reshape(2, size, COLS)

    lane = iota((SLOTS, COLS), 1)
    first = (iota((8, 128), 1) == 0).astype(F32).astype(BF16)
    pairs = [(j, n) for j in range(2) for n in range(3)]
    alive, alive_row, scores, vals = [], [], {}, []
    for j in range(2):
        marks = a_v[j, :, :, :, 0:128].reshape(SLOTS, 128)
        alive.append(marks[:, 0:1].astype(F32) > -4.0)
        mark = lax.dot_general(first, marks, LAST, preferred_element_type=F32)
        alive_row.append((mark > -4.0).astype(F32).astype(BF16))
    for j, n in pairs:
        keys = k_v[j]
        mine = (lane >= n * HD) & (lane < (n + 1) * HD)
        head_keys = jnp.where(mine, keys, jnp.zeros_like(keys))
        scores[j, n] = lax.dot_general(head_keys, q_v[j], LAST, preferred_element_type=F32)
    for j in range(2):
        rows = a_v[j].reshape(SLOTS, D)
        made = lax.dot_general(wv_v[...], rows, LAST, preferred_element_type=F32)
        vals.append(made.astype(BF16))
    parts = {}
    for j, n in pairs:
        masked = scores[j, n] * (HD ** -0.5) + jnp.where(alive[j], 0.0, -1e30)
        top = jnp.max(masked, axis=0, keepdims=True)
        weights = jnp.exp(masked - top)
        inverse = 1.0 / jnp.sum(weights, axis=0, keepdims=True)
        part = jnp.dot(
            vals[j][n * HD : (n + 1) * HD], weights.astype(BF16), preferred_element_type=F32
        )
        parts[j, n] = (part * inverse).astype(BF16)
    mixed = [jnp.concatenate([parts[j, n] for n in range(3)], axis=0) for j in range(2)]
    pooled = jnp.zeros((8, COLS), F32)
    for j in range(2):
        total = lax.dot_general(alive_row[j], mixed[j], LAST, preferred_element_type=F32)
        pooled = jnp.where(iota((8, COLS), 0) == j, total / counts[j], pooled)
    partial = jnp.dot(pooled.astype(BF16), wo_v[...], preferred_element_type=F32)
    for i in range(NX):
        s_v[i, :, 0:COLS] = partial[:, i * COLS : (i + 1) * COLS]
        s_v[i, :, COLS:256] = jnp.zeros((8, 256 - COLS), F32)
    p_sends = []
    for o in range(1, NX):
        to = (h + o) % NX
        copy = pltpu.make_async_remote_copy(
            src_ref=s_v.at[to],
            dst_ref=r_v.at[o - 1],
            send_sem=ps_sem.at[o - 1],
            recv_sem=pr_sem.at[o - 1],
            device_id={"dp": dp, "head": to},
            device_id_type=MESH,
        )
        copy.start()
        p_sends.append(copy)
    for j in range(2):
        ordered = jnp.where(alive[j], perm_v[...].astype(F32), 0.0).astype(BF16)
        result = jnp.dot(mixed[j], ordered, preferred_element_type=F32)
        mixed_out[j] = result.astype(BF16)
    for copy in x_sends[-7:]:
        copy.wait_send()
    pl.when(y != h)(local_sends[-1].wait_send)
    own_part = s_v[h]
    for copy in p_sends:
        copy.wait_recv()
    everything = own_part + r_v[0] + r_v[1] + r_v[2]
    region_out[...] = everything[0:2, 0:COLS].astype(BF16)
    for copy in p_sends:
        copy.wait_send()


def local(
    tile_features, tile_weight, tile_bias, query_weight, key_weight, value_weight, output_weight,
    tile_region, region_block, region_count,
):
    dma = pltpu.SemaphoreType.DMA
    anywhere = pl.BlockSpec(memory_space=pl.ANY)
    mixed, region = pl.pallas_call(
        kernel,
        out_shape=(
            pltpu.VMEM((2, COLS, SLOTS), BF16),
            pltpu.VMEM((2, COLS), BF16),
        ),
        in_specs=[anywhere] * 10,
        out_specs=(pl.BlockSpec(memory_space=pltpu.VMEM), pl.BlockSpec(memory_space=pltpu.VMEM)),
        scratch_shapes=[
            pltpu.VMEM((PAD, D), BF16),
            pltpu.VMEM((D, D), BF16),
            pltpu.VMEM((D,), F32),
            pltpu.VMEM((COLS, D), BF16),
            pltpu.VMEM((COLS, D), BF16),
            pltpu.VMEM((COLS, D), BF16),
            pltpu.VMEM((COLS, D), BF16),
            pltpu.VMEM((16, 128), jnp.int32),
            pltpu.VMEM((1, 256), jnp.int32),
            pltpu.VMEM((1, 256), jnp.int32),
            pltpu.VMEM((NZ, NG, D), BF16),
            pltpu.VMEM((NZ, NG, D), BF16),
            pltpu.VMEM((2, NG, D), BF16),
            pltpu.VMEM((1, NG, D), BF16),
            pltpu.VMEM((CHUNKS, 2, 2, 2 * CHUNK, D), BF16),
            pltpu.VMEM((2, CHUNKS, NG, 2 * CHUNK, D), BF16),
            pltpu.VMEM((2, SLOTS, COLS), BF16),
            pltpu.VMEM((2, SLOTS, COLS), BF16),
            pltpu.VMEM((SLOTS, SLOTS), BF16),
            pltpu.VMEM((NX, 8, 256), F32),
            pltpu.VMEM((NX - 1, 8, 256), F32),
            dma((10,)),
            dma,
            dma((NZ + 1,)),
            dma((NZ,)),
            dma((2,)),
            dma((CHUNKS, NX, 2)),
            dma((CHUNKS, NG)),
            dma((NX - 1,)),
            dma((NX - 1,)),
        ],
        compiler_params=pltpu.CompilerParams(
            collective_id=0, has_side_effects=True, vmem_limit_bytes=60 * 1024 * 1024
        ),
        name="regroup_attend",
    )(
        tile_features, tile_weight, tile_bias, query_weight.T, key_weight.T, value_weight.T,
        output_weight, tile_region.reshape(TILE, 128), region_block.reshape(1, 256),
        region_count.reshape(1, 256),
    )
    return mixed.transpose(0, 2, 1), region


def solution(mesh):
    in_specs = (
        P("dp", None),
        P(),
        P(),
        P(None, "head"),
        P(None, "head"),
        P(None, "head"),
        P("head", None),
        P(),
        P(),
        P(),
    )
    out_specs = (P("dp", None, "head"), P("dp", "head"))
    return jax.shard_map(local, mesh=mesh, in_specs=in_specs, out_specs=out_specs, check_vma=False)
```

```python
import functools

import jax
import jax.numpy as jnp
from jax import lax
from jax.experimental import pallas as pl
from jax.experimental.pallas import tpu as pltpu
from jax.sharding import PartitionSpec as P

D = 768
SLOTS = 256
HD = 64
COLS = 192
TILE = 352
PAD = 384
NZ, NG, NX = 16, 8, 4
EMPTY = -8.0
MESH = pl.DeviceIdType.MESH
F32 = jnp.float32
BF16 = jnp.bfloat16
LAST = (((1,), (1,)), ((), ()))
CHUNK = 4
CHUNKS = NZ // CHUNK
OFFSETS = (0, 1, 15, 2, 14, 3, 13, 4, 12, 5, 11, 6, 10, 7, 9, 8)
DIRECT = (1, 15, 2, 14, 3, 13, 4, 12, 5, 11, 6, 10)


def iota(shape, dim):
    return lax.broadcasted_iota(jnp.int32, shape, dim)


def kernel(
    feat, w, bias, wq, wk, wv, wo, reg, blk, cnt,
    mixed_out, region_out,
    f_v, w_v, bias_v, wq_v, wk_v, wv_v, wo_v, reg_v, blk_v, cnt_v,
    e_v, z_v, up_v, down_v, c_v, a_v, q_v, k_v, perm_v, s_v, r_v,
    in_sem, own_sem, zs_sem, zr_sem, relay_sem, xs_sem, xr_sem, ps_sem, pr_sem,
):
    dp = lax.axis_index("dp")
    h = lax.axis_index("head")
    z = dp // NG
    g = dp % NG
    y = g // 2
    core = g % 2

    first_row = (dp * TILE) // 128
    lane_off = (dp * TILE) % 128
    reg_base = pl.multiple_of(jnp.minimum((first_row // 8) * 8, TILE - 16), 8)
    loads = [
        pltpu.make_async_copy(reg.at[pl.ds(reg_base, 16)], reg_v, in_sem.at[0]),
        pltpu.make_async_copy(blk, blk_v, in_sem.at[1]),
        pltpu.make_async_copy(feat, f_v.at[pl.ds(0, TILE)], in_sem.at[2]),
        pltpu.make_async_copy(w, w_v, in_sem.at[3]),
        pltpu.make_async_copy(bias, bias_v, in_sem.at[4]),
        pltpu.make_async_copy(wq, wq_v, in_sem.at[5]),
        pltpu.make_async_copy(wk, wk_v, in_sem.at[6]),
        pltpu.make_async_copy(wv, wv_v, in_sem.at[7]),
        pltpu.make_async_copy(wo, wo_v, in_sem.at[8]),
        pltpu.make_async_copy(cnt, cnt_v, in_sem.at[9]),
    ]
    barrier = pltpu.get_barrier_semaphore()
    for o in reversed(DIRECT):
        pl.semaphore_signal(
            barrier, inc=1, device_id={"dp": ((z + o) % NZ) * NG + g, "head": h}, device_id_type=MESH
        )
    for o in range(NG):
        source = (g + o) % NG
        if o == 0:
            @pl.when(y != h)
            def _():
                pl.semaphore_signal(
                    barrier, inc=1, device_id={"dp": dp, "head": y}, device_id_type=MESH
                )
        else:
            pl.semaphore_signal(
                barrier, inc=1, device_id={"dp": z * NG + source, "head": y}, device_id_type=MESH
            )
    for o in range(1, NX):
        pl.semaphore_signal(
            barrier, inc=1, device_id={"dp": dp, "head": (h + o) % NX}, device_id_type=MESH
        )
    for load in loads:
        load.start()

    f_v[pl.ds(TILE, PAD - TILE), :] = jnp.zeros((PAD - TILE, D), BF16)
    upper = (iota((PAD, PAD), 0) < iota((PAD, PAD), 1)).astype(F32).astype(BF16)
    loads[0].wait()
    loads[1].wait()
    parts = []
    for i in range(4):
        at = jnp.minimum(first_row + i, TILE - 1) - reg_base
        parts.append(reg_v[pl.ds(at, 1), :])
    line = jnp.broadcast_to(jnp.concatenate(parts, axis=1), (8, 512))
    line = pltpu.roll(line, (512 - lane_off) % 512, 1)[:, :PAD]
    in_range = iota((8, PAD), 1) < TILE
    line = jnp.where(in_range, line, -1)
    hot = (iota((256, PAD), 0) == line[0:1, :]).astype(F32)
    hot16 = hot.astype(BF16)
    block_row = jnp.broadcast_to(blk_v[...].astype(F32), (8, 256)).astype(BF16)
    block = jnp.dot(block_row, hot16, preferred_element_type=F32)
    before = jnp.dot(hot16, upper, preferred_element_type=F32)
    rank = jnp.sum(before * hot, axis=0, keepdims=True)
    code = jnp.where(in_range[0:1, :], block[0:1, :] * 2.0 + rank, -1.0)
    row = iota((128, PAD), 0)
    target = (32 * ((z + row // NG) % NZ) + 8 * h + row % NG).astype(F32)
    pick = (code == target).astype(F32)
    live = jnp.sum(pick, axis=1, keepdims=True)
    loads[2].wait()
    x = jnp.dot(pick.astype(BF16), f_v[...], preferred_element_type=F32).astype(BF16)
    loads[3].wait()
    loads[4].wait()
    hidden = jnp.dot(x, w_v[...], preferred_element_type=F32) + bias_v[...].reshape(1, D)
    embedded = jax.nn.gelu(hidden, approximate=True)
    embedded = jnp.where(live > 0.5, embedded, EMPTY).astype(BF16)
    e_v[...] = embedded.reshape(NZ, NG, D)

    pl.semaphore_wait(barrier, NG + len(DIRECT) + NX - 1 - (y == h).astype(jnp.int32))

    def along_z(source, target, away, sent, got):
        copy = pltpu.make_async_remote_copy(
            src_ref=source,
            dst_ref=target,
            send_sem=zs_sem.at[sent],
            recv_sem=got,
            device_id={"dp": ((z + away) % NZ) * NG + g, "head": h},
            device_id_type=MESH,
        )
        copy.start()
        return copy

    up = along_z(e_v.at[pl.ds(7, 2)], up_v, 3, 0, relay_sem.at[0])
    down = along_z(e_v.at[pl.ds(9, 1)], down_v, 13, NZ, relay_sem.at[1])
    z_sends = {}
    for k in DIRECT:
        p = OFFSETS.index(NZ - k)
        z_sends[p] = along_z(e_v.at[k], z_v.at[p], k, p, zr_sem.at[p])
    own = pltpu.make_async_copy(e_v.at[0], z_v.at[0], own_sem)
    own.start()

    at = iota((SLOTS, SLOTS), 0)
    slot = iota((SLOTS, SLOTS), 1)
    place = (at // 64) * CHUNK + at % CHUNK
    off = jnp.zeros((SLOTS, SLOTS), jnp.int32)
    for p in range(1, NZ):
        off = jnp.where(place == p, OFFSETS[p], off)
    to_slot = (((z + off) % NZ) * NG + at // 8 % NG) * 2 + at // CHUNK % 2
    perm_v[...] = (slot == to_slot).astype(F32).astype(BF16)

    rows = 8 * CHUNK
    out_row = iota((rows, rows), 0)
    in_row = (out_row % CHUNK) * 8 + out_row // 8 % 2 * 2 + out_row // 16 * 4 + out_row // CHUNK % 2
    order = (iota((rows, rows), 1) == in_row).astype(F32).astype(BF16)
    x_sends = []
    local_sends = []
    for n in range(CHUNKS):
        if n == 1:
            up.wait_recv()
            down.wait_recv()
            for source, away, offset in ((up_v.at[1], 5, 8), (up_v.at[0], 4, 9), (down_v.at[0], 12, 7)):
                p = OFFSETS.index(offset)
                z_sends[p] = along_z(source, z_v.at[p], away, p, zr_sem.at[p])
        for p in range(n * CHUNK, (n + 1) * CHUNK):
            if p == 0:
                own.wait()
            else:
                z_sends[p].wait_recv()
        arrived = z_v[n * CHUNK : (n + 1) * CHUNK].reshape(rows, D)
        turned = jnp.dot(order, arrived, preferred_element_type=F32).astype(BF16)
        c_v[n] = turned.reshape(2, 2, 2 * CHUNK, D)
        for o in (2, 1, 3, 0):
            for oc in (1, 0):
                to = (h + o) % NX
                to_core = (core + oc) % 2
                copy = pltpu.make_async_remote_copy(
                    src_ref=c_v.at[n, to_core],
                    dst_ref=a_v.at[:, n, g],
                    send_sem=xs_sem.at[n, o, oc],
                    recv_sem=xr_sem.at[n, g],
                    device_id={"dp": z * NG + h * 2 + to_core, "head": to},
                    device_id_type=MESH,
                )
                if o == 0 and oc == 0:
                    here = pltpu.make_async_copy(
                        c_v.at[n, to_core], a_v.at[:, n, g], xr_sem.at[n, g]
                    )
                    pl.when(y == h)(here.start)
                    pl.when(y != h)(copy.start)
                    local_sends.append(copy)
                else:
                    copy.start()
                    x_sends.append(copy)

    for load in loads[5:]:
        load.wait()
    counts = []
    for j in range(2):
        here = blk_v[...] == dp * 2 + j
        counts.append(
            jnp.sum(jnp.where(here, cnt_v[...].astype(F32), 0.0), axis=1, keepdims=True)
        )
    size = 16 * CHUNK
    for n in range(CHUNKS):
        if n == CHUNKS - 1:
            for copy in (up, down, *z_sends.values()):
                copy.wait_send()
            for copy in x_sends[:-7]:
                copy.wait_send()
            for copy in local_sends[:-1]:
                pl.when(y != h)(copy.wait_send)
        for source in range(NG):
            landed = a_v.at[:, n, source]
            pltpu.make_async_copy(landed, landed, xr_sem.at[n, source]).wait()
        rows = a_v[:, n].reshape(2 * size, D)
        for weight, kept in ((wk_v, k_v), (wq_v, q_v)):
            made = lax.dot_general(rows, weight[...], LAST, preferred_element_type=F32)
            kept[:, n * size : (n + 1) * size] = made.astype(BF16).reshape(2, size, COLS)

    first = (iota((8, 128), 1) == 0).astype(F32).astype(BF16)
    pairs = [(j, n) for j in range(2) for n in range(3)]
    alive, alive_row, scores, vals = [], [], {}, []
    for j in range(2):
        marks = a_v[j, :, :, :, 0:128].reshape(SLOTS, 128)
        alive.append(marks[:, 0:1].astype(F32) > -4.0)
        mark = lax.dot_general(first, marks, LAST, preferred_element_type=F32)
        alive_row.append((mark > -4.0).astype(F32).astype(BF16))
    for j, n in pairs:
        scores[j, n] = lax.dot_general(
            k_v[j, :, n * HD : (n + 1) * HD], q_v[j, :, n * HD : (n + 1) * HD], LAST,
            preferred_element_type=F32,
        )
    for j in range(2):
        rows = a_v[j].reshape(SLOTS, D)
        made = lax.dot_general(wv_v[...], rows, LAST, preferred_element_type=F32)
        vals.append(made.astype(BF16))
    parts = {}
    for j, n in pairs:
        masked = scores[j, n] * (HD ** -0.5) + jnp.where(alive[j], 0.0, -1e30)
        top = jnp.max(masked, axis=0, keepdims=True)
        weights = jnp.exp(masked - top)
        inverse = 1.0 / jnp.sum(weights, axis=0, keepdims=True)
        part = jnp.dot(
            vals[j][n * HD : (n + 1) * HD], weights.astype(BF16), preferred_element_type=F32
        )
        parts[j, n] = (part * inverse).astype(BF16)
    mixed = [jnp.concatenate([parts[j, n] for n in range(3)], axis=0) for j in range(2)]
    pooled = jnp.zeros((8, COLS), F32)
    for j in range(2):
        total = lax.dot_general(alive_row[j], mixed[j], LAST, preferred_element_type=F32)
        pooled = jnp.where(iota((8, COLS), 0) == j, total / counts[j], pooled)
    partial = jnp.dot(pooled.astype(BF16), wo_v[...], preferred_element_type=F32)
    for i in range(NX):
        s_v[i, :, 0:COLS] = partial[:, i * COLS : (i + 1) * COLS]
        s_v[i, :, COLS:256] = jnp.zeros((8, 256 - COLS), F32)
    p_sends = []
    for o in range(1, NX):
        to = (h + o) % NX
        copy = pltpu.make_async_remote_copy(
            src_ref=s_v.at[to],
            dst_ref=r_v.at[o - 1],
            send_sem=ps_sem.at[o - 1],
            recv_sem=pr_sem.at[o - 1],
            device_id={"dp": dp, "head": to},
            device_id_type=MESH,
        )
        copy.start()
        p_sends.append(copy)
    for j in range(2):
        ordered = jnp.where(alive[j], perm_v[...].astype(F32), 0.0).astype(BF16)
        result = jnp.dot(mixed[j], ordered, preferred_element_type=F32)
        mixed_out[j] = result.astype(BF16)
    for copy in x_sends[-7:]:
        copy.wait_send()
    pl.when(y != h)(local_sends[-1].wait_send)
    own_part = s_v[h]
    for copy in p_sends:
        copy.wait_recv()
    everything = own_part + r_v[0] + r_v[1] + r_v[2]
    region_out[...] = everything[0:2, 0:COLS].astype(BF16)
    for copy in p_sends:
        copy.wait_send()


def local(
    tile_features, tile_weight, tile_bias, query_weight, key_weight, value_weight, output_weight,
    tile_region, region_block, region_count,
):
    dma = pltpu.SemaphoreType.DMA
    anywhere = pl.BlockSpec(memory_space=pl.ANY)
    mixed, region = pl.pallas_call(
        kernel,
        out_shape=(
            pltpu.VMEM((2, COLS, SLOTS), BF16),
            pltpu.VMEM((2, COLS), BF16),
        ),
        in_specs=[anywhere] * 10,
        out_specs=(pl.BlockSpec(memory_space=pltpu.VMEM), pl.BlockSpec(memory_space=pltpu.VMEM)),
        scratch_shapes=[
            pltpu.VMEM((PAD, D), BF16),
            pltpu.VMEM((D, D), BF16),
            pltpu.VMEM((D,), F32),
            pltpu.VMEM((COLS, D), BF16),
            pltpu.VMEM((COLS, D), BF16),
            pltpu.VMEM((COLS, D), BF16),
            pltpu.VMEM((COLS, D), BF16),
            pltpu.VMEM((16, 128), jnp.int32),
            pltpu.VMEM((1, 256), jnp.int32),
            pltpu.VMEM((1, 256), jnp.int32),
            pltpu.VMEM((NZ, NG, D), BF16),
            pltpu.VMEM((NZ, NG, D), BF16),
            pltpu.VMEM((2, NG, D), BF16),
            pltpu.VMEM((1, NG, D), BF16),
            pltpu.VMEM((CHUNKS, 2, 2, 2 * CHUNK, D), BF16),
            pltpu.VMEM((2, CHUNKS, NG, 2 * CHUNK, D), BF16),
            pltpu.VMEM((2, SLOTS, COLS), BF16),
            pltpu.VMEM((2, SLOTS, COLS), BF16),
            pltpu.VMEM((SLOTS, SLOTS), BF16),
            pltpu.VMEM((NX, 8, 256), F32),
            pltpu.VMEM((NX - 1, 8, 256), F32),
            dma((10,)),
            dma,
            dma((NZ + 1,)),
            dma((NZ,)),
            dma((2,)),
            dma((CHUNKS, NX, 2)),
            dma((CHUNKS, NG)),
            dma((NX - 1,)),
            dma((NX - 1,)),
        ],
        compiler_params=pltpu.CompilerParams(
            collective_id=0, has_side_effects=True, vmem_limit_bytes=60 * 1024 * 1024
        ),
        name="regroup_attend",
    )(
        tile_features, tile_weight, tile_bias, query_weight.T, key_weight.T, value_weight.T,
        output_weight, tile_region.reshape(TILE, 128), region_block.reshape(1, 256),
        region_count.reshape(1, 256),
    )
    return mixed.transpose(0, 2, 1), region


def solution(mesh):
    in_specs = (
        P("dp", None),
        P(),
        P(),
        P(None, "head"),
        P(None, "head"),
        P(None, "head"),
        P("head", None),
        P(),
        P(),
        P(),
    )
    out_specs = (P("dp", None, "head"), P("dp", "head"))
    return jax.shard_map(local, mesh=mesh, in_specs=in_specs, out_specs=out_specs, check_vma=False)
```

```python
import functools

import jax
import jax.numpy as jnp
from jax import lax
from jax.experimental import pallas as pl
from jax.experimental.pallas import tpu as pltpu
from jax.sharding import PartitionSpec as P

D = 768
SLOTS = 256
HD = 64
COLS = 192
TILE = 352
PAD = 384
NZ, NG, NX = 16, 8, 4
EMPTY = -8.0
MESH = pl.DeviceIdType.MESH
F32 = jnp.float32
BF16 = jnp.bfloat16
LAST = (((1,), (1,)), ((), ()))
CHUNK = 4
CHUNKS = NZ // CHUNK
OFFSETS = (0, 1, 15, 2, 14, 3, 13, 4, 12, 5, 11, 6, 10, 7, 9, 8)
DIRECT = (1, 15, 2, 14, 3, 13, 4, 12, 5, 11)


def iota(shape, dim):
    return lax.broadcasted_iota(jnp.int32, shape, dim)


def kernel(
    feat, w, bias, wq, wk, wv, wo, reg, blk, cnt,
    mixed_out, region_out,
    f_v, w_v, bias_v, wq_v, wk_v, wv_v, wo_v, reg_v, blk_v, cnt_v,
    e_v, z_v, up_v, down_v, c_v, a_v, q_v, k_v, perm_v, s_v, r_v,
    in_sem, own_sem, zs_sem, zr_sem, relay_sem, xs_sem, xr_sem, ps_sem, pr_sem,
):
    dp = lax.axis_index("dp")
    h = lax.axis_index("head")
    z = dp // NG
    g = dp % NG
    y = g // 2
    core = g % 2

    first_row = (dp * TILE) // 128
    lane_off = (dp * TILE) % 128
    reg_base = pl.multiple_of(jnp.minimum((first_row // 8) * 8, TILE - 16), 8)
    loads = [
        pltpu.make_async_copy(reg.at[pl.ds(reg_base, 16)], reg_v, in_sem.at[0]),
        pltpu.make_async_copy(blk, blk_v, in_sem.at[1]),
        pltpu.make_async_copy(feat, f_v.at[pl.ds(0, TILE)], in_sem.at[2]),
        pltpu.make_async_copy(w, w_v, in_sem.at[3]),
        pltpu.make_async_copy(bias, bias_v, in_sem.at[4]),
        pltpu.make_async_copy(wq, wq_v, in_sem.at[5]),
        pltpu.make_async_copy(wk, wk_v, in_sem.at[6]),
        pltpu.make_async_copy(wv, wv_v, in_sem.at[7]),
        pltpu.make_async_copy(wo, wo_v, in_sem.at[8]),
        pltpu.make_async_copy(cnt, cnt_v, in_sem.at[9]),
    ]
    barrier = pltpu.get_barrier_semaphore()
    for o in reversed(DIRECT):
        pl.semaphore_signal(
            barrier, inc=1, device_id={"dp": ((z + o) % NZ) * NG + g, "head": h}, device_id_type=MESH
        )
    for o in range(NG):
        source = (g + o) % NG
        if o == 0:
            @pl.when(y != h)
            def _():
                pl.semaphore_signal(
                    barrier, inc=1, device_id={"dp": dp, "head": y}, device_id_type=MESH
                )
        else:
            pl.semaphore_signal(
                barrier, inc=1, device_id={"dp": z * NG + source, "head": y}, device_id_type=MESH
            )
    for o in range(1, NX):
        pl.semaphore_signal(
            barrier, inc=1, device_id={"dp": dp, "head": (h + o) % NX}, device_id_type=MESH
        )
    for load in loads:
        load.start()

    f_v[pl.ds(TILE, PAD - TILE), :] = jnp.zeros((PAD - TILE, D), BF16)
    upper = (iota((PAD, PAD), 0) < iota((PAD, PAD), 1)).astype(F32).astype(BF16)
    loads[0].wait()
    loads[1].wait()
    parts = []
    for i in range(4):
        at = jnp.minimum(first_row + i, TILE - 1) - reg_base
        parts.append(reg_v[pl.ds(at, 1), :])
    line = jnp.broadcast_to(jnp.concatenate(parts, axis=1), (8, 512))
    line = pltpu.roll(line, (512 - lane_off) % 512, 1)[:, :PAD]
    in_range = iota((8, PAD), 1) < TILE
    line = jnp.where(in_range, line, -1)
    hot = (iota((256, PAD), 0) == line[0:1, :]).astype(F32)
    hot16 = hot.astype(BF16)
    block_row = jnp.broadcast_to(blk_v[...].astype(F32), (8, 256)).astype(BF16)
    block = jnp.dot(block_row, hot16, preferred_element_type=F32)
    before = jnp.dot(hot16, upper, preferred_element_type=F32)
    rank = jnp.sum(before * hot, axis=0, keepdims=True)
    code = jnp.where(in_range[0:1, :], block[0:1, :] * 2.0 + rank, -1.0)
    row = iota((128, PAD), 0)
    target = (32 * ((z + row // NG) % NZ) + 8 * h + row % NG).astype(F32)
    pick = (code == target).astype(F32)
    live = jnp.sum(pick, axis=1, keepdims=True)
    loads[2].wait()
    x = jnp.dot(pick.astype(BF16), f_v[...], preferred_element_type=F32).astype(BF16)
    loads[3].wait()
    loads[4].wait()
    hidden = jnp.dot(x, w_v[...], preferred_element_type=F32) + bias_v[...].reshape(1, D)
    embedded = jax.nn.gelu(hidden, approximate=True)
    embedded = jnp.where(live > 0.5, embedded, EMPTY).astype(BF16)
    e_v[...] = embedded.reshape(NZ, NG, D)

    pl.semaphore_wait(barrier, NG + len(DIRECT) + NX - 1 - (y == h).astype(jnp.int32))

    def along_z(source, target, away, sent, got):
        copy = pltpu.make_async_remote_copy(
            src_ref=source,
            dst_ref=target,
            send_sem=zs_sem.at[sent],
            recv_sem=got,
            device_id={"dp": ((z + away) % NZ) * NG + g, "head": h},
            device_id_type=MESH,
        )
        copy.start()
        return copy

    up = along_z(e_v.at[pl.ds(6, 3)], up_v, 3, 0, relay_sem.at[0])
    down = along_z(e_v.at[pl.ds(9, 2)], down_v, 13, NZ, relay_sem.at[1])
    z_sends = {}
    for k in DIRECT:
        p = OFFSETS.index(NZ - k)
        z_sends[p] = along_z(e_v.at[k], z_v.at[p], k, p, zr_sem.at[p])
    own = pltpu.make_async_copy(e_v.at[0], z_v.at[0], own_sem)
    own.start()

    at = iota((SLOTS, SLOTS), 0)
    slot = iota((SLOTS, SLOTS), 1)
    place = (at // 64) * CHUNK + at % CHUNK
    off = jnp.zeros((SLOTS, SLOTS), jnp.int32)
    for p in range(1, NZ):
        off = jnp.where(place == p, OFFSETS[p], off)
    to_slot = (((z + off) % NZ) * NG + at // 8 % NG) * 2 + at // CHUNK % 2
    perm_v[...] = (slot == to_slot).astype(F32).astype(BF16)

    rows = 8 * CHUNK
    out_row = iota((rows, rows), 0)
    in_row = (out_row % CHUNK) * 8 + out_row // 8 % 2 * 2 + out_row // 16 * 4 + out_row // CHUNK % 2
    order = (iota((rows, rows), 1) == in_row).astype(F32).astype(BF16)
    x_sends = []
    local_sends = []
    for n in range(CHUNKS):
        if n == 1:
            up.wait_recv()
            down.wait_recv()
            for source, away, offset in ((up_v.at[2], 5, 8), (up_v.at[1], 4, 9), (up_v.at[0], 3, 10), (down_v.at[0], 12, 7), (down_v.at[1], 13, 6)):
                p = OFFSETS.index(offset)
                z_sends[p] = along_z(source, z_v.at[p], away, p, zr_sem.at[p])
        for p in range(n * CHUNK, (n + 1) * CHUNK):
            if p == 0:
                own.wait()
            else:
                z_sends[p].wait_recv()
        arrived = z_v[n * CHUNK : (n + 1) * CHUNK].reshape(rows, D)
        turned = jnp.dot(order, arrived, preferred_element_type=F32).astype(BF16)
        c_v[n] = turned.reshape(2, 2, 2 * CHUNK, D)
        for o in (2, 1, 3, 0):
            for oc in (1, 0):
                to = (h + o) % NX
                to_core = (core + oc) % 2
                copy = pltpu.make_async_remote_copy(
                    src_ref=c_v.at[n, to_core],
                    dst_ref=a_v.at[:, n, g],
                    send_sem=xs_sem.at[n, o, oc],
                    recv_sem=xr_sem.at[n, g],
                    device_id={"dp": z * NG + h * 2 + to_core, "head": to},
                    device_id_type=MESH,
                )
                if o == 0 and oc == 0:
                    here = pltpu.make_async_copy(
                        c_v.at[n, to_core], a_v.at[:, n, g], xr_sem.at[n, g]
                    )
                    pl.when(y == h)(here.start)
                    pl.when(y != h)(copy.start)
                    local_sends.append(copy)
                else:
                    copy.start()
                    x_sends.append(copy)

    for load in loads[5:]:
        load.wait()
    counts = []
    for j in range(2):
        here = blk_v[...] == dp * 2 + j
        counts.append(
            jnp.sum(jnp.where(here, cnt_v[...].astype(F32), 0.0), axis=1, keepdims=True)
        )
    size = 16 * CHUNK
    for n in range(CHUNKS):
        if n == CHUNKS - 1:
            for copy in (up, down, *z_sends.values()):
                copy.wait_send()
            for copy in x_sends[:-7]:
                copy.wait_send()
            for copy in local_sends[:-1]:
                pl.when(y != h)(copy.wait_send)
        for source in range(NG):
            landed = a_v.at[:, n, source]
            pltpu.make_async_copy(landed, landed, xr_sem.at[n, source]).wait()
        rows = a_v[:, n].reshape(2 * size, D)
        for weight, kept in ((wk_v, k_v), (wq_v, q_v)):
            made = lax.dot_general(rows, weight[...], LAST, preferred_element_type=F32)
            kept[:, n * size : (n + 1) * size] = made.astype(BF16).reshape(2, size, COLS)

    first = (iota((8, 128), 1) == 0).astype(F32).astype(BF16)
    pairs = [(j, n) for j in range(2) for n in range(3)]
    alive, alive_row, scores, vals = [], [], {}, []
    for j in range(2):
        marks = a_v[j, :, :, :, 0:128].reshape(SLOTS, 128)
        alive.append(marks[:, 0:1].astype(F32) > -4.0)
        mark = lax.dot_general(first, marks, LAST, preferred_element_type=F32)
        alive_row.append((mark > -4.0).astype(F32).astype(BF16))
    for j, n in pairs:
        scores[j, n] = lax.dot_general(
            k_v[j, :, n * HD : (n + 1) * HD], q_v[j, :, n * HD : (n + 1) * HD], LAST,
            preferred_element_type=F32,
        )
    for j in range(2):
        rows = a_v[j].reshape(SLOTS, D)
        made = lax.dot_general(wv_v[...], rows, LAST, preferred_element_type=F32)
        vals.append(made.astype(BF16))
    parts = {}
    for j, n in pairs:
        masked = scores[j, n] * (HD ** -0.5) + jnp.where(alive[j], 0.0, -1e30)
        top = jnp.max(masked, axis=0, keepdims=True)
        weights = jnp.exp(masked - top)
        inverse = 1.0 / jnp.sum(weights, axis=0, keepdims=True)
        part = jnp.dot(
            vals[j][n * HD : (n + 1) * HD], weights.astype(BF16), preferred_element_type=F32
        )
        parts[j, n] = (part * inverse).astype(BF16)
    mixed = [jnp.concatenate([parts[j, n] for n in range(3)], axis=0) for j in range(2)]
    pooled = jnp.zeros((8, COLS), F32)
    for j in range(2):
        total = lax.dot_general(alive_row[j], mixed[j], LAST, preferred_element_type=F32)
        pooled = jnp.where(iota((8, COLS), 0) == j, total / counts[j], pooled)
    partial = jnp.dot(pooled.astype(BF16), wo_v[...], preferred_element_type=F32)
    for i in range(NX):
        s_v[i, :, 0:COLS] = partial[:, i * COLS : (i + 1) * COLS]
        s_v[i, :, COLS:256] = jnp.zeros((8, 256 - COLS), F32)
    p_sends = []
    for o in range(1, NX):
        to = (h + o) % NX
        copy = pltpu.make_async_remote_copy(
            src_ref=s_v.at[to],
            dst_ref=r_v.at[o - 1],
            send_sem=ps_sem.at[o - 1],
            recv_sem=pr_sem.at[o - 1],
            device_id={"dp": dp, "head": to},
            device_id_type=MESH,
        )
        copy.start()
        p_sends.append(copy)
    for j in range(2):
        ordered = jnp.where(alive[j], perm_v[...].astype(F32), 0.0).astype(BF16)
        result = jnp.dot(mixed[j], ordered, preferred_element_type=F32)
        mixed_out[j] = result.astype(BF16)
    for copy in x_sends[-7:]:
        copy.wait_send()
    pl.when(y != h)(local_sends[-1].wait_send)
    own_part = s_v[h]
    for copy in p_sends:
        copy.wait_recv()
    everything = own_part + r_v[0] + r_v[1] + r_v[2]
    region_out[...] = everything[0:2, 0:COLS].astype(BF16)
    for copy in p_sends:
        copy.wait_send()


def local(
    tile_features, tile_weight, tile_bias, query_weight, key_weight, value_weight, output_weight,
    tile_region, region_block, region_count,
):
    dma = pltpu.SemaphoreType.DMA
    anywhere = pl.BlockSpec(memory_space=pl.ANY)
    mixed, region = pl.pallas_call(
        kernel,
        out_shape=(
            pltpu.VMEM((2, COLS, SLOTS), BF16),
            pltpu.VMEM((2, COLS), BF16),
        ),
        in_specs=[anywhere] * 10,
        out_specs=(pl.BlockSpec(memory_space=pltpu.VMEM), pl.BlockSpec(memory_space=pltpu.VMEM)),
        scratch_shapes=[
            pltpu.VMEM((PAD, D), BF16),
            pltpu.VMEM((D, D), BF16),
            pltpu.VMEM((D,), F32),
            pltpu.VMEM((COLS, D), BF16),
            pltpu.VMEM((COLS, D), BF16),
            pltpu.VMEM((COLS, D), BF16),
            pltpu.VMEM((COLS, D), BF16),
            pltpu.VMEM((16, 128), jnp.int32),
            pltpu.VMEM((1, 256), jnp.int32),
            pltpu.VMEM((1, 256), jnp.int32),
            pltpu.VMEM((NZ, NG, D), BF16),
            pltpu.VMEM((NZ, NG, D), BF16),
            pltpu.VMEM((3, NG, D), BF16),
            pltpu.VMEM((2, NG, D), BF16),
            pltpu.VMEM((CHUNKS, 2, 2, 2 * CHUNK, D), BF16),
            pltpu.VMEM((2, CHUNKS, NG, 2 * CHUNK, D), BF16),
            pltpu.VMEM((2, SLOTS, COLS), BF16),
            pltpu.VMEM((2, SLOTS, COLS), BF16),
            pltpu.VMEM((SLOTS, SLOTS), BF16),
            pltpu.VMEM((NX, 8, 256), F32),
            pltpu.VMEM((NX - 1, 8, 256), F32),
            dma((10,)),
            dma,
            dma((NZ + 1,)),
            dma((NZ,)),
            dma((2,)),
            dma((CHUNKS, NX, 2)),
            dma((CHUNKS, NG)),
            dma((NX - 1,)),
            dma((NX - 1,)),
        ],
        compiler_params=pltpu.CompilerParams(
            collective_id=0, has_side_effects=True, vmem_limit_bytes=60 * 1024 * 1024
        ),
        name="regroup_attend",
    )(
        tile_features, tile_weight, tile_bias, query_weight.T, key_weight.T, value_weight.T,
        output_weight, tile_region.reshape(TILE, 128), region_block.reshape(1, 256),
        region_count.reshape(1, 256),
    )
    return mixed.transpose(0, 2, 1), region


def solution(mesh):
    in_specs = (
        P("dp", None),
        P(),
        P(),
        P(None, "head"),
        P(None, "head"),
        P(None, "head"),
        P("head", None),
        P(),
        P(),
        P(),
    )
    out_specs = (P("dp", None, "head"), P("dp", "head"))
    return jax.shard_map(local, mesh=mesh, in_specs=in_specs, out_specs=out_specs, check_vma=False)
```
